128 devices in a mesh: head: 8 (over z, core), inner: 4 (over x), outer: 4 (over y).
Axes of the slice: x: 4, y: 4, z: 4, core: 2. Of those that a mesh axis runs over, the one named last changes fastest.
Arguments:
- query_in: bfloat16 [32768, 2048], P(('inner', 'outer'), 'head'), may hold values from -6 to 6
- key_in: bfloat16 [32768, 2048], P(('inner', 'outer'), 'head'), may hold values from -5 to 5
- value_in: bfloat16 [32768, 4096], P(('inner', 'outer'), 'head'), may hold values from -6 to 6
- log_decay: float32 [32768, 32], P(('inner', 'outer'), 'head'), may hold values from -1 to 0
- beta_gate: float32 [32768, 32], P(('inner', 'outer'), 'head'), may hold values from 0.6 to 1
- conv_query: bfloat16 [4, 2048], P(None, 'head'), may hold values from -2.5 to 2.5
- conv_key: bfloat16 [4, 2048], P(None, 'head'), may hold values from -2.5 to 2.5
- conv_value: bfloat16 [4, 4096], P(None, 'head'), may hold values from -2.5 to 2.5
- norm_gain: float32 [4096], P('head'), may hold values from 0.25 to 1.75
Outputs:
- layer_out: bfloat16 [32768, 4096], P(('inner', 'outer'), 'head')
The draws below stay inside these ranges and needn't reach their ends.
All inputs are finite; a program needn't handle non-finite values.
Results may differ from the reference program's by a relative error of at most 0.002.
Values may be sent and summed in bfloat16 or wider, within the bound.
No kernel may reach another device: no remote copies, remote signals or barrier semaphores. Data moves between devices by JAX's collectives and lax.ppermute only.
A program may use at most 128 MiB of HBM per device.

```python
import jax
import jax.numpy as jnp
from jax import lax

HK = 16
HV = 32
DK = 128
DV = 128
CONV = 4
STRETCH = 64
TOK_DEV = 2048
CONTEXT_TOKENS = 32768


def draw_key_in(key, part):
    key = jax.random.fold_in(key, 11)
    mask_key = jax.random.fold_in(key, 1)
    value_key = jax.random.fold_in(key, 2)
    orders = jax.vmap(lambda sub_key: jax.random.permutation(sub_key, DK))(jax.random.split(mask_key, HK))
    weak_mask = orders < DK // 2
    base_vals = jnp.clip(jax.random.normal(value_key, (CONTEXT_TOKENS, HK, DK), jnp.float32), -5.0, 5.0)
    weak_scale = 0.1
    scaled = base_vals * jnp.where(weak_mask, weak_scale, 1.0)[None]
    return scaled.reshape(CONTEXT_TOKENS, HK * DK).astype(jnp.bfloat16)


def draw_log_decay(key, part):
    key = jax.random.fold_in(key, 23)
    random_subkeys = jax.random.split(key, 7)
    slow_share = 0.5
    slow_mask = jax.random.uniform(random_subkeys[0], (HV,), jnp.float32) < slow_share
    slow_rate = jnp.exp(jax.random.uniform(random_subkeys[1], (HV,), jnp.float32, jnp.log(0.05), jnp.log(0.5))) / CONTEXT_TOKENS
    fast_rate = jnp.exp(jax.random.uniform(random_subkeys[2], (HV,), jnp.float32, jnp.log(1.0 / 60.0), jnp.log(1.0 / 10.0)))
    head_decay_rate = jnp.where(slow_mask, slow_rate, fast_rate)
    coarse_portion = jax.random.uniform(random_subkeys[3], (CONTEXT_TOKENS, HV), jnp.float32, 0.5, 1.5)
    block_total = CONTEXT_TOKENS // TOK_DEV
    block_extent = jnp.exp(jax.random.uniform(random_subkeys[4], (block_total, HV), jnp.float32, jnp.log(0.5), jnp.log(2.0)))
    block_extent = jnp.repeat(block_extent, TOK_DEV, axis=0)
    surge_position = jax.random.randint(random_subkeys[5], (2,), 0, CONTEXT_TOKENS)
    surge_extent = jnp.log(jax.random.uniform(random_subkeys[6], (2,), jnp.float32, 0.6, 0.8))
    token_positions = jnp.arange(CONTEXT_TOKENS)
    surge_logits = jnp.where(token_positions == surge_position[0], surge_extent[0], 0.0) + jnp.where(token_positions == surge_position[1], surge_extent[1], 0.0)
    return -head_decay_rate[None, :] * coarse_portion * block_extent + surge_logits[:, None]


def block_scale(key, shape, cuts, low, high):
    def one(dim, parts):
        steps = jax.random.uniform(jax.random.fold_in(jax.random.fold_in(key, 6), dim), (parts,), jnp.float32, low / len(cuts), high / len(cuts))
        return jnp.repeat(jnp.exp(steps), shape[dim] // parts).reshape((-1,) + (1,) * (len(shape) - dim - 1))

    level = one(*cuts[0])
    for cut in cuts[1:]:
        level = level * one(*cut)
    return level


def scatter_about(stream_key, shape, scale, most, shards=(), kind=jnp.bfloat16):
    values = scale * jax.random.normal(stream_key, shape, jnp.float32)
    if shards:
        values = values * block_scale(stream_key, shape, shards, -0.22, 0.18)
    return jnp.clip(values, -most, most).astype(kind)


def setup_inputs(seed: int = 0) -> dict:
    keys = jax.random.split(jax.random.key(seed), 10)
    query_in = scatter_about(keys[0], (CONTEXT_TOKENS, HK * DK), 1.0, 6.0, ((0, 16), (1, 8)))
    key_in = draw_key_in(jax.random.fold_in(keys[9], 71), 0)
    value_in = scatter_about(keys[2], (CONTEXT_TOKENS, HV * DV), 1.0, 6.0, ((0, 16), (1, 8)))
    log_decay = draw_log_decay(jax.random.fold_in(keys[9], 71), 0)
    beta_gate = jnp.clip(0.6 + 0.39999998 * jax.random.uniform(keys[4], (CONTEXT_TOKENS, HV), jnp.float32) ** block_scale(keys[4], (CONTEXT_TOKENS, HV), ((0, 16), (1, 8)), -0.2, 0.2), 0.6, 1.0)
    conv_query = scatter_about(keys[5], (CONV, HK * DK), 0.5, 2.5, ((1, 8),))
    conv_key = scatter_about(keys[6], (CONV, HK * DK), 0.5, 2.5, ((1, 8),))
    conv_value = scatter_about(keys[7], (CONV, HV * DV), 0.5, 2.5, ((1, 8),))
    norm_gain = jnp.clip(1.0 + 0.15 * jax.random.normal(keys[8], (HV * DV,), jnp.float32), 0.25, 1.75)
    return dict(query_in=query_in, key_in=key_in, value_in=value_in, log_decay=log_decay, beta_gate=beta_gate, conv_query=conv_query, conv_key=conv_key, conv_value=conv_value, norm_gain=norm_gain)


highest = lax.Precision.HIGHEST

def product(pattern, left_op, right_op):
    return jnp.einsum(pattern, left_op, right_op, precision=highest)

def causal_conv(source, rim_rows, weight):
    extended = jnp.concatenate([rim_rows, source], axis=0).astype(jnp.float32)
    tap_weights = weight.astype(jnp.float32)
    tok_rows = source.shape[0]
    summed = tap_weights[0] * extended[0:tok_rows]
    for tap_index in range(1, tap_weights.shape[0]):
        summed = summed + tap_weights[tap_index] * extended[tap_index:tap_index + tok_rows]
    return jax.nn.silu(summed)

def stretch_parts(queries, keys_unit, values, log_gates, beta_gates):
    block_len = log_gates.shape[-1]
    cumulative = jnp.cumsum(log_gates, axis=-1)
    row_ids = lax.broadcasted_iota(jnp.int32, (block_len, block_len), 0)
    col_ids = lax.broadcasted_iota(jnp.int32, (block_len, block_len), 1)
    lower_mask = row_ids >= col_ids
    strict_mask = row_ids > col_ids
    gap_log = cumulative[..., :, None] - cumulative[..., None, :]
    decay_mat = jnp.where(lower_mask, jnp.exp(jnp.where(lower_mask, gap_log, 0.0)), 0.0)
    key_grams = product('...cd,...ed->...ce', keys_unit, keys_unit)
    strict_mat = jnp.where(strict_mask, key_grams * decay_mat, 0.0) * beta_gates[..., :, None]
    unit_mat = jnp.eye(block_len, dtype=jnp.float32)
    right_side = beta_gates[..., None] * jnp.concatenate([keys_unit * jnp.exp(cumulative)[..., None], values], axis=-1)
    solved = lax.linalg.triangular_solve(unit_mat + strict_mat, right_side, left_side=True, lower=True, unit_diagonal=True)
    key_width = keys_unit.shape[-1]
    wy_keys = solved[..., :key_width]
    wy_values = solved[..., key_width:]
    q_decayed = queries * jnp.exp(cumulative)[..., None]
    qk_decayed = product('...cd,...ed->...ce', queries, keys_unit) * decay_mat
    k_decayed = keys_unit * jnp.exp(cumulative[..., -1:] - cumulative)[..., None]
    stretch_decay = jnp.exp(cumulative[..., -1])
    return (wy_keys, wy_values, q_decayed, qk_decayed, k_decayed, stretch_decay)

def head_run(inputs):
    queries, keys_unit, values, log_gates, beta_gates = inputs
    terms = stretch_parts(queries, keys_unit, values, log_gates, beta_gates)

    def step_stretch(running, stretch_in):
        wy_keys, wy_values, q_decayed, qk_decayed, k_decayed, stretch_decay = stretch_in
        new_values = wy_values - product('cd,de->ce', wy_keys, running)
        emitted = product('cd,de->ce', q_decayed, running) + product('ce,ed->cd', qk_decayed, new_values)
        running = stretch_decay * running + product('cd,ce->de', k_decayed, new_values)
        return (running, emitted)
    empty_state = jnp.zeros((keys_unit.shape[-1], values.shape[-1]), jnp.float32)
    final_state, emitted = lax.scan(step_stretch, empty_state, terms)
    return emitted

def reference(query_in, key_in, value_in, log_decay, beta_gate, conv_query, conv_key, conv_value, norm_gain):
    tok_rows = query_in.shape[0]
    head_group = HV // HK
    query_feat = causal_conv(query_in, jnp.zeros((CONV - 1, query_in.shape[1]), query_in.dtype), conv_query)
    key_feat = causal_conv(key_in, jnp.zeros((CONV - 1, key_in.shape[1]), key_in.dtype), conv_key)
    value_feat = causal_conv(value_in, jnp.zeros((CONV - 1, value_in.shape[1]), value_in.dtype), conv_value)
    keys_unit = key_feat.reshape(tok_rows, HK, DK)
    keys_unit = keys_unit / jnp.sqrt(lax.optimization_barrier(jnp.sum(keys_unit * keys_unit, axis=-1, keepdims=True)) + 1e-06)
    keys_unit = jnp.repeat(keys_unit, head_group, axis=1)
    queries = jnp.repeat(query_feat.reshape(tok_rows, HK, DK), head_group, axis=1)
    values = value_feat.reshape(tok_rows, HV, DV)

    def blocked(feature):
        return jnp.transpose(feature, (1, 0, 2)).reshape(feature.shape[1], tok_rows // STRETCH, STRETCH, feature.shape[2])

    def gate_blocks(gates):
        return jnp.transpose(gates).reshape(gates.shape[1], tok_rows // STRETCH, STRETCH)
    emitted = lax.map(head_run, (blocked(queries), blocked(keys_unit), blocked(values), gate_blocks(log_decay), gate_blocks(beta_gate)))
    recurrent = jnp.transpose(emitted, (1, 2, 0, 3)).reshape(tok_rows, HV, DV)
    inv_rms = 1.0 / jnp.sqrt(lax.optimization_barrier(jnp.mean(recurrent * recurrent, axis=-1, keepdims=True)) + 1e-06)
    gain_rows = norm_gain.reshape(HV, DV)
    return (recurrent * inv_rms * gain_rows).reshape(tok_rows, HV * DV).astype(jnp.bfloat16)
```

```python
import jax
import jax.numpy as jnp
from jax import lax
from jax.experimental import pallas as pl
from jax.experimental.pallas import tpu as pltpu
from jax.sharding import PartitionSpec as P

DK = 128
DV = 128
CONV = 4
SPAN = 256
HALF = 128
BASE = 16
VMEM_BYTES = 56 * 1024 * 1024

f32 = jnp.float32
bf16 = jnp.bfloat16


def shifted(value, axis, steps, wrap):
    count = lax.axis_size(axis)
    if wrap:
        pairs = [(source, (source + steps) % count) for source in range(count)]
    else:
        pairs = [(source, source + steps) for source in range(count - steps)]
    return lax.ppermute(value, axis, pairs)


def split(value):
    high = value.astype(bf16)
    return high, (value - high.astype(f32)).astype(bf16)


def dot(left, right):
    return jnp.dot(left, right, preferred_element_type=f32)


def beside(*parts):
    return jnp.concatenate(parts, axis=1)


def above(*parts):
    return jnp.concatenate(parts, axis=0)


def product(left, right):
    if left[0].shape[1] == HALF:
        return dot(beside(*left), above(right[0], right[0])) + dot(left[0], right[1])
    return dot(left[0], right[0]) + dot(left[1], right[0]) + dot(left[0], right[1])


def product_small(left, right):
    pair = beside(*right)
    both = dot(beside(*left), above(pair, pair))
    return both[:, :HALF] + both[:, HALF:]


def iotas(shape):
    return lax.broadcasted_iota(jnp.int32, shape, 0), lax.broadcasted_iota(jnp.int32, shape, 1)


def conv_silu(halo_ref, prev_ref, cur_ref, taps_ref, first):
    prev = jnp.where(first, halo_ref[...].astype(f32), prev_ref[...].astype(f32))
    cur = cur_ref[...].astype(f32)
    taps = taps_ref[...].astype(f32)
    extended = above(prev[8:], cur)
    rows = cur.shape[0]
    total = taps[CONV - 1 : CONV] * cur
    for tap in range(CONV - 1):
        start = 8 - (CONV - 1) + tap
        total = total + taps[tap : tap + 1] * extended[start : start + rows]
    return total / (1.0 + jnp.exp(-total))


def decay_blocks(cum_col, cum_row, strict):
    row_ids, col_ids = iotas((HALF, HALF))
    keep = (row_ids > col_ids) if strict else (row_ids >= col_ids)
    top = jnp.exp(jnp.where(keep, cum_col[:HALF] - cum_row[:, :HALF], -1e30))
    low = jnp.exp(cum_col[HALF:] - cum_row[:, :HALF])
    end = jnp.exp(jnp.where(keep, cum_col[HALF:] - cum_row[:, HALF:], -1e30))
    return top, low, end


def state_kernel(
    turn_ref, key_ref, key_prev, key_halo, val_ref, val_prev, val_halo, gate_ref, key_taps, val_taps,
    keyt_out, solved_out, start_out, row_out, col_out, end0, end1, end2, end3,
    run_ref, map_ref, add_ref, fin_ref, level_ref, pick_ref, tri_ref,
):
    step = pl.program_id(0)
    heads = run_ref.shape[0]
    key_heads = key_ref.shape[1] // DK
    group = heads // key_heads
    row_ids, col_ids = iotas((HALF, HALF))
    unit = jnp.where(row_ids == col_ids, 1.0, 0.0).astype(f32)
    base_mask = (row_ids // BASE) == (col_ids // BASE)

    @pl.when(step == 0)
    def _():
        zeros = jnp.zeros((HALF, HALF), f32)
        for head in range(heads):
            run_ref[head, 0] = beside(zeros, unit).astype(bf16)
            run_ref[head, 1] = beside(zeros, zeros).astype(bf16)
            map_ref[head] = beside(unit, zeros).astype(bf16)
            add_ref[head] = zeros
        size = BASE
        for level in range(level_ref.shape[0]):
            picked = (
                (row_ids // (2 * size) == col_ids // (2 * size))
                & (row_ids % (2 * size) >= size)
                & (col_ids % (2 * size) < size)
            )
            level_ref[level] = jnp.where(picked, 1.0, 0.0).astype(bf16)
            size *= 2
        for place in range(BASE - 1):
            chosen = jnp.where(row_ids == (col_ids // BASE) * BASE + place, 1.0, 0.0).astype(bf16)
            pick_ref[:, place * HALF : (place + 1) * HALF] = above(chosen, chosen)
        tri_rows, tri_cols = iotas((SPAN, SPAN))
        tri_ref[...] = jnp.where(tri_rows <= tri_cols, 1.0, 0.0).astype(bf16)

    def advance(head):
        maps = map_ref[head]
        high, low = run_ref[head, 0], run_ref[head, 1]
        moved = dot(maps, above(high, high)) + dot(maps[:, :DK], low)
        return beside(moved[:, :DV] + add_ref[head], moved[:, DV:])

    for head in range(heads):
        high, low = split(advance(head))
        run_ref[head, 0] = high
        run_ref[head, 1] = low
        start_out[0, head, 0] = high
        start_out[0, head, 1] = low

    gates = gate_ref[...]
    is_log = lax.broadcasted_iota(jnp.int32, gates.shape, 0) < heads
    logs = jnp.where(is_log, gates, 0.0)
    logs = above(logs, logs)
    high = logs.astype(bf16)
    rest = logs - high.astype(f32)
    mid = rest.astype(bf16)
    low = (rest - mid.astype(f32)).astype(bf16)
    tri = tri_ref[...]
    cum = (dot(high, tri) + dot(mid, tri) + dot(low, tri))[: gates.shape[0]]
    row_out[...] = cum
    packed = above(
        jnp.where(is_log, cum, gates),
        jnp.exp(cum),
        jnp.zeros((HALF - 2 * gates.shape[0], SPAN), f32),
    )
    cols = packed.T
    col_out[...] = cols

    first = step == 0
    key_feat = conv_silu(key_halo, key_prev, key_ref, key_taps, first)
    val_feat = conv_silu(val_halo, val_prev, val_ref, val_taps, first)

    keys, keys_t, grams = [], [], []
    for key_head in range(key_heads):
        feat = key_feat[:, key_head * DK : (key_head + 1) * DK]
        keyed = feat * lax.rsqrt(jnp.sum(feat * feat, axis=1, keepdims=True) + 1e-6)
        turned = keyed.T
        parts = split(turned)
        keyt_out[0, key_head, 0] = parts[0]
        keyt_out[0, key_head, 1] = parts[1]
        keys.append(keyed)
        keys_t.append(turned)
        grams.append(product(split(keyed), parts))

    diag, below = [], []
    for head in range(heads):
        gram = grams[head // group]
        beta_col = cols[:, heads + head : heads + head + 1]
        top, low, end = decay_blocks(cols[:, head : head + 1], cum[head : head + 1], True)
        diag.append(gram[:HALF, :HALF] * top * beta_col[:HALF])
        below.append(split(gram[HALF:, :HALF] * low * beta_col[HALF:]))
        diag.append(gram[HALF:, HALF:] * end * beta_col[HALF:])

    blocks = HALF // BASE
    compact = above(
        *(jnp.sum(jnp.where(base_mask, item, 0.0).reshape(blocks, BASE, HALF), axis=0) for item in diag)
    )
    spread = dot(beside(*split(compact)), pick_ref[...])
    count = len(diag)
    within = lax.broadcasted_iota(jnp.int32, (count, BASE, HALF), 1)
    lanes = lax.broadcasted_iota(jnp.int32, (count, BASE, HALF), 2)
    small = jnp.where(within == lanes % BASE, 1.0, 0.0).astype(f32)
    for place in range(BASE - 1):
        factor = spread[:, place * HALF : (place + 1) * HALF].reshape(count, BASE, HALF)
        small = small - factor * small[:, place : place + 1, :]
    inverses = [
        jnp.where(base_mask, jnp.broadcast_to(small[item][None], (blocks, BASE, HALF)).reshape(HALF, HALF), 0.0)
        for item in range(count)
    ]
    diag_parts = [split(item) for item in diag]
    for level in range(level_ref.shape[0]):
        mask = level_ref[level]
        inv_parts = [split(item) for item in inverses]
        inner = [
            product_small((item[0] * mask, item[1] * mask), inv)
            for item, inv in zip(diag_parts, inv_parts)
        ]
        inverses = [
            whole - product_small(inv, split(part))
            for whole, inv, part in zip(inverses, inv_parts, inner)
        ]
    inv_parts = [split(item) for item in inverses]

    right, tops, lows = [], [], []
    for head in range(heads):
        beta_col = cols[:, heads + head : heads + head + 1]
        exp_col = cols[:, 2 * heads + head : 2 * heads + head + 1]
        right.append(
            beside(keys[head // group] * (beta_col * exp_col), val_feat[:, head * DV : (head + 1) * DV] * beta_col)
        )
    for head in range(heads):
        tops.append(split(product(inv_parts[2 * head], split(right[head][:HALF]))))
    for head in range(heads):
        rest = right[head][HALF:] - product(below[head], tops[head])
        lows.append(split(product(inv_parts[2 * head + 1], split(rest))))
    for head in range(heads):
        solved = (above(tops[head][0], lows[head][0]), above(tops[head][1], lows[head][1]))
        solved_out[0, head, 0] = solved[0]
        solved_out[0, head, 1] = solved[1]
        cum_row = cum[head : head + 1]
        last = cum_row[:, SPAN - 1 : SPAN]
        faded = split(keys_t[head // group] * jnp.exp(last - cum_row))
        gathered = product(faded, solved)
        maps = unit * jnp.exp(last) - gathered[:, :DK]
        map_ref[head] = beside(*split(maps))
        add_ref[head] = gathered[:, DK:]

    @pl.when(step == pl.num_programs(0) - 1)
    def _():
        for head in range(heads):
            fin_ref[head] = advance(head)
        turn = turn_ref[0]
        for place, end_ref in enumerate((end0, end1, end2, end3)):
            end_ref[...] = fin_ref[lax.rem(turn + place, heads)]


def query_kernel(
    query_ref, query_prev, query_halo, taps_ref, keyt_ref, solved_ref, start_ref, row_ref, col_ref, *rest
):
    local_out, carry_out = rest[-3:-1]
    offset = rest[-1]
    first = pl.program_id(0) + offset == 0
    feat = conv_silu(query_halo, query_prev, query_ref, taps_ref, first)
    key_heads = query_ref.shape[1] // DK
    heads = solved_ref.shape[1]
    group = heads // key_heads
    queries, grams = [], []
    for key_head in range(key_heads):
        query = feat[:, key_head * DK : (key_head + 1) * DK]
        queries.append(query)
        grams.append(product(split(query), (keyt_ref[0, key_head, 0], keyt_ref[0, key_head, 1])))
    lifted = []
    for head in range(heads):
        gram = grams[head // group]
        top, low, end = decay_blocks(col_ref[:, head : head + 1], row_ref[head : head + 1], False)
        high, fine = solved_ref[0, head, 0], solved_ref[0, head, 1]
        upper = product(split(gram[:HALF, :HALF] * top), (high[:HALF], fine[:HALF]))
        wide = beside(gram[HALF:, :HALF] * low, gram[HALF:, HALF:] * end)
        lifted.append(above(upper, product(split(wide), (high, fine))))
    for head in range(heads):
        exp_col = col_ref[:, 2 * heads + head : 2 * heads + head + 1]
        reach = queries[head // group] * exp_col - lifted[head][:, :DK]
        seen = product(split(reach), (start_ref[0, head, 0], start_ref[0, head, 1]))
        local_out[:, head * DV : (head + 1) * DV] = seen[:, :DV] + lifted[head][:, DK:]
        carry_out[:, head * 2 * DK : (head + 1) * 2 * DK] = beside(*split(seen[:, DV:]))


def compose_kernel(turn_ref, part0, part1, part2, part3, total_out, tail_out, prefix_out, all_ref):
    count = all_ref.shape[0]
    turn = turn_ref[0]
    for place, part in enumerate((part0, part1, part2, part3)):
        all_ref[lax.rem(turn + count - place, count)] = part[...]
    running = all_ref[0]
    prefix_out[0] = running
    for member in range(1, count):
        own = all_ref[member]
        moved = product(split(own[:, DV:]), split(running))
        running = beside(moved[:, :DV] + own[:, :DV], moved[:, DV:])
        if member < count - 1:
            prefix_out[member] = running
    total_out[...] = running
    tail_out[...] = running[:, :DV]


def enter_kernel(turn_ref, near_ref, next_ref, far_ref, prefix_ref, out0, out1, out2, out3, all_ref):
    count = all_ref.shape[0]
    turn = turn_ref[0]
    far = next_ref[:, :DV] + product_small(split(next_ref[:, DV:]), split(far_ref[...]))
    entry = near_ref[:, :DV] + product_small(split(near_ref[:, DV:]), split(far))
    parts = split(entry)
    all_ref[0] = entry
    for member in range(1, count):
        prefix = prefix_ref[member - 1]
        all_ref[member] = prefix[:, :DV] + product_small(split(prefix[:, DV:]), parts)
    for place, out in enumerate((out0, out1, out2, out3)):
        out[...] = all_ref[lax.rem(turn + place, count)]


def close_kernel(turn_ref, part0, part1, part2, part3, local_ref, carry_ref, gain_ref, out_ref, state_ref):
    heads = state_ref.shape[0]
    turn = turn_ref[0]

    @pl.when(pl.program_id(0) == 0)
    def _():
        for place, part in enumerate((part0, part1, part2, part3)):
            pair = beside(*split(part[...]))
            state_ref[lax.rem(turn + heads - place, heads)] = above(pair, pair)

    for head in range(heads):
        both = dot(carry_ref[:, head * 2 * DK : (head + 1) * 2 * DK], state_ref[head])
        value = local_ref[:, head * DV : (head + 1) * DV] + both[:, :DV] + both[:, DV:]
        scale = lax.rsqrt(jnp.sum(value * value, axis=1, keepdims=True) * (1.0 / DV) + 1e-6)
        gain = gain_ref[:, head * DV : (head + 1) * DV]
        out_ref[:, head * DV : (head + 1) * DV] = (value * scale * gain).astype(bf16)


def whole(shape):
    return pl.BlockSpec(shape, lambda *_: (0,) * len(shape))


def params():
    return pltpu.CompilerParams(dimension_semantics=("arbitrary",), vmem_limit_bytes=VMEM_BYTES)


def cost(flops, size, exps=0):
    return pl.CostEstimate(flops=flops, bytes_accessed=size, transcendentals=exps)


def per_device(
    query_in, key_in, value_in, log_decay, beta_gate, conv_query, conv_key, conv_value, norm_gain
):
    tok_rows, query_width = query_in.shape
    value_width = value_in.shape[1]
    key_heads = query_width // DK
    heads = value_width // DV
    spans = tok_rows // SPAN
    turn = lax.axis_index("outer").astype(jnp.int32).reshape(1)
    tails = beside(query_in[tok_rows - 16 :], key_in[tok_rows - 16 :], value_in[tok_rows - 16 :])
    before = shifted(tails, ("inner", "outer"), 1, False)
    query_halo = before[:, :query_width]
    key_halo = before[:, query_width : 2 * query_width]
    value_halo = before[:, 2 * query_width :]
    gates = above(log_decay.T, beta_gate.T)

    def prev_rows(offset):
        return lambda i, *_: (jnp.maximum((i + offset) * (SPAN // 16) - 1, 0), 0)

    square = jax.ShapeDtypeStruct((DK, 2 * DV), f32)
    keyt, solved, starts, rows, cols, *ends = pl.pallas_call(
        state_kernel,
        grid_spec=pltpu.PrefetchScalarGridSpec(
            num_scalar_prefetch=1,
            grid=(spans,),
            in_specs=[
                pl.BlockSpec((SPAN, query_width), lambda i, *_: (i, 0)),
                pl.BlockSpec((16, query_width), prev_rows(0)),
                whole((16, query_width)),
                pl.BlockSpec((SPAN, value_width), lambda i, *_: (i, 0)),
                pl.BlockSpec((16, value_width), prev_rows(0)),
                whole((16, value_width)),
                pl.BlockSpec((2 * heads, SPAN), lambda i, *_: (0, i)),
                whole((CONV, query_width)),
                whole((CONV, value_width)),
            ],
            out_specs=[
                pl.BlockSpec((1, key_heads, 2, DK, SPAN), lambda i, *_: (i, 0, 0, 0, 0)),
                pl.BlockSpec((1, heads, 2, SPAN, 2 * DV), lambda i, *_: (i, 0, 0, 0, 0)),
                pl.BlockSpec((1, heads, 2, DK, 2 * DV), lambda i, *_: (i, 0, 0, 0, 0)),
                pl.BlockSpec((2 * heads, SPAN), lambda i, *_: (0, i)),
                pl.BlockSpec((SPAN, HALF), lambda i, *_: (i, 0)),
            ]
            + [whole((DK, 2 * DV))] * 4,
            scratch_shapes=[
                pltpu.VMEM((heads, 2, DK, 2 * DV), bf16),
                pltpu.VMEM((heads, DK, 2 * DK), bf16),
                pltpu.VMEM((heads, DK, DV), f32),
                pltpu.VMEM((heads, DK, 2 * DV), f32),
                pltpu.VMEM((3, HALF, HALF), bf16),
                pltpu.VMEM((2 * HALF, (BASE - 1) * HALF), bf16),
                pltpu.VMEM((SPAN, SPAN), bf16),
            ],
        ),
        out_shape=[
            jax.ShapeDtypeStruct((spans, key_heads, 2, DK, SPAN), bf16),
            jax.ShapeDtypeStruct((spans, heads, 2, SPAN, 2 * DV), bf16),
            jax.ShapeDtypeStruct((spans, heads, 2, DK, 2 * DV), bf16),
            jax.ShapeDtypeStruct((2 * heads, tok_rows), f32),
            jax.ShapeDtypeStruct((tok_rows, HALF), f32),
        ]
        + [square] * 4,
        compiler_params=params(),
        cost_estimate=cost(20_000_000_000, 20_000_000),
        name="state_path",
    )(turn, key_in, key_in, key_halo, value_in, value_in, value_halo, gates, conv_key, conv_value)

    parts = [ends[0]] + [shifted(ends[k], "outer", k, True) for k in (1, 2, 3)]

    out_types = (
        jax.ShapeDtypeStruct((tok_rows, value_width), f32),
        jax.ShapeDtypeStruct((tok_rows, 2 * value_width), bf16),
    )

    def query_part(offset, count, earlier):
        def body(*refs):
            query_kernel(*refs, offset)

        def at(i):
            return i + offset

        return pl.pallas_call(
            body,
            grid=(count,),
            in_specs=[
                pl.BlockSpec((SPAN, query_width), lambda i: (at(i), 0)),
                pl.BlockSpec((16, query_width), prev_rows(offset)),
                whole((16, query_width)),
                whole((CONV, query_width)),
                pl.BlockSpec((1, key_heads, 2, DK, SPAN), lambda i: (at(i), 0, 0, 0, 0)),
                pl.BlockSpec((1, heads, 2, SPAN, 2 * DV), lambda i: (at(i), 0, 0, 0, 0)),
                pl.BlockSpec((1, heads, 2, DK, 2 * DV), lambda i: (at(i), 0, 0, 0, 0)),
                pl.BlockSpec((2 * heads, SPAN), lambda i: (0, at(i))),
                pl.BlockSpec((SPAN, HALF), lambda i: (at(i), 0)),
            ]
            + [pl.BlockSpec(memory_space=pl.ANY)] * len(earlier),
            out_specs=[
                pl.BlockSpec((SPAN, value_width), lambda i: (at(i), 0)),
                pl.BlockSpec((SPAN, 2 * value_width), lambda i: (at(i), 0)),
            ],
            out_shape=out_types,
            input_output_aliases={9 + k: k for k in range(len(earlier))},
            compiler_params=params(),
            cost_estimate=cost(2_000_000_000 * count, 3_000_000 * count),
            name="query_path",
        )(query_in, query_in, query_halo, conv_query, keyt, solved, starts, rows, cols, *earlier)

    first_half = query_part(0, spans // 2, ())

    total, tail, prefix = pl.pallas_call(
        compose_kernel,
        grid_spec=pltpu.PrefetchScalarGridSpec(
            num_scalar_prefetch=1,
            grid=(1,),
            in_specs=[whole((DK, 2 * DV))] * 4,
            out_specs=[whole((DK, 2 * DV)), whole((DK, DV)), whole((3, DK, 2 * DV))],
            scratch_shapes=[pltpu.VMEM((4, DK, 2 * DV), f32)],
        ),
        out_shape=[
            square,
            jax.ShapeDtypeStruct((DK, DV), f32),
            jax.ShapeDtypeStruct((3, DK, 2 * DV), f32),
        ],
        compiler_params=params(),
        cost_estimate=cost(100_000_000, 1_000_000),
        name="compose",
    )(turn, *parts)
    near = shifted(total, "inner", 1, False)
    middle = shifted(total, "inner", 2, False)
    far = shifted(tail, "inner", 3, False)

    local, carry = query_part(spans // 2, spans - spans // 2, first_half)

    entries = pl.pallas_call(
        enter_kernel,
        grid_spec=pltpu.PrefetchScalarGridSpec(
            num_scalar_prefetch=1,
            grid=(1,),
            in_specs=[whole((DK, 2 * DV)), whole((DK, 2 * DV)), whole((DK, DV)), whole((3, DK, 2 * DV))],
            out_specs=[whole((DK, DV))] * 4,
            scratch_shapes=[pltpu.VMEM((4, DK, DV), f32)],
        ),
        out_shape=[jax.ShapeDtypeStruct((DK, DV), f32)] * 4,
        compiler_params=params(),
        cost_estimate=cost(50_000_000, 1_000_000),
        name="enter",
    )(turn, near, middle, far, prefix)
    states = [entries[0]] + [shifted(entries[k], "outer", k, True) for k in (1, 2, 3)]

    return pl.pallas_call(
        close_kernel,
        grid_spec=pltpu.PrefetchScalarGridSpec(
            num_scalar_prefetch=1,
            grid=(spans,),
            in_specs=[whole((DK, DV))] * 4
            + [
                pl.BlockSpec((SPAN, value_width), lambda i, *_: (i, 0)),
                pl.BlockSpec((SPAN, 2 * value_width), lambda i, *_: (i, 0)),
                whole((1, value_width)),
            ],
            out_specs=pl.BlockSpec((SPAN, value_width), lambda i, *_: (i, 0)),
            scratch_shapes=[pltpu.VMEM((heads, 2 * DK, 2 * DV), bf16)],
        ),
        out_shape=jax.ShapeDtypeStruct((tok_rows, value_width), bf16),
        compiler_params=params(),
        cost_estimate=cost(2_000_000_000, 10_000_000),
        name="close",
    )(turn, *states, local, carry, norm_gain.reshape(1, value_width))


def solution(mesh):
    in_specs = (
        P(("inner", "outer"), "head"),
        P(("inner", "outer"), "head"),
        P(("inner", "outer"), "head"),
        P(("inner", "outer"), "head"),
        P(("inner", "outer"), "head"),
        P(None, "head"),
        P(None, "head"),
        P(None, "head"),
        P("head"),
    )
    out_specs = P(("inner", "outer"), "head")
    return jax.shard_map(
        per_device, mesh=mesh, in_specs=in_specs, out_specs=out_specs, check_vma=False
    )
```

```python
import jax
import jax.numpy as jnp
from jax import lax
from jax.experimental import pallas as pl
from jax.experimental.pallas import tpu as pltpu
from jax.sharding import PartitionSpec as P

DK = 128
DV = 128
CONV = 4
SPAN = 256
HALF = 128
BASE = 16
MIB = 1024 * 1024
STATE_MIB = 16

f32 = jnp.float32
bf16 = jnp.bfloat16


def shifted(value, axis, steps, wrap):
    count = lax.axis_size(axis)
    if wrap:
        pairs = [(source, (source + steps) % count) for source in range(count)]
    else:
        pairs = [(source, source + steps) for source in range(count - steps)]
    return lax.ppermute(value, axis, pairs)


def split(value):
    high = value.astype(bf16)
    return high, (value - high.astype(f32)).astype(bf16)


def dot(left, right):
    return jnp.dot(left, right, preferred_element_type=f32)


def beside(*parts):
    return jnp.concatenate(parts, axis=1)


def above(*parts):
    return jnp.concatenate(parts, axis=0)


def product(left, right):
    if left[0].shape[1] == HALF:
        return dot(beside(*left), above(right[0], right[0])) + dot(left[0], right[1])
    return dot(left[0], right[0]) + dot(left[1], right[0]) + dot(left[0], right[1])


def product_small(left, right):
    return dot(beside(*left), above(right[0], right[0])) + dot(left[0], right[1])


def odd_rows(value, size):
    return above(*(value[start : start + size] for start in range(size, value.shape[0], 2 * size)))


def spread_rows(value, size):
    gap = jnp.zeros((size, value.shape[1]), value.dtype)
    return above(*(part for start in range(0, value.shape[0], size) for part in (gap, value[start : start + size])))


def merge_rows(value, odd, size):
    return above(
        *(
            part
            for start in range(0, odd.shape[0], size)
            for part in (value[2 * start : 2 * start + size], odd[start : start + size])
        )
    )


def iotas(shape):
    return lax.broadcasted_iota(jnp.int32, shape, 0), lax.broadcasted_iota(jnp.int32, shape, 1)


def conv_silu(halo_ref, prev_ref, cur_ref, taps_ref, first):
    prev = jnp.where(first, halo_ref[...].astype(f32), prev_ref[...].astype(f32))
    cur = cur_ref[...].astype(f32)
    taps = taps_ref[...].astype(f32)
    extended = above(prev[8:], cur)
    rows = cur.shape[0]
    total = taps[CONV - 1 : CONV] * cur
    for tap in range(CONV - 1):
        start = 8 - (CONV - 1) + tap
        total = total + taps[tap : tap + 1] * extended[start : start + rows]
    return total / (1.0 + jnp.exp(-total))


def decay_blocks(cum_col, cum_row, strict):
    row_ids, col_ids = iotas((HALF, HALF))
    keep = (row_ids > col_ids) if strict else (row_ids >= col_ids)
    top = jnp.exp(jnp.where(keep, cum_col[:HALF] - cum_row[:, :HALF], -1e30))
    low = jnp.exp(cum_col[HALF:] - cum_row[:, :HALF])
    end = jnp.exp(jnp.where(keep, cum_col[HALF:] - cum_row[:, HALF:], -1e30))
    return top, low, end


def state_kernel(
    turn_ref, key_ref, key_prev, key_halo, val_ref, val_prev, val_halo, gate_ref, key_taps, val_taps,
    keyt_out, solved_out, start_out, row_out, col_out, end0, end1, end2, end3,
    run_ref, map_ref, add_ref, fin_ref, level_ref, pick_ref, tri_ref,
):
    step = pl.program_id(0)
    heads = run_ref.shape[0]
    key_heads = key_ref.shape[1] // DK
    group = heads // key_heads
    row_ids, col_ids = iotas((HALF, HALF))
    unit = jnp.where(row_ids == col_ids, 1.0, 0.0).astype(f32)
    base_mask = (row_ids // BASE) == (col_ids // BASE)

    @pl.when(step == 0)
    def _():
        zeros = jnp.zeros((HALF, HALF), f32)
        for head in range(heads):
            run_ref[head, 0] = beside(zeros, unit).astype(bf16)
            run_ref[head, 1] = beside(zeros, zeros).astype(bf16)
            map_ref[head] = beside(unit, zeros).astype(bf16)
            add_ref[head] = zeros
        size = BASE
        for level in range(level_ref.shape[0]):
            picked = (
                (row_ids // (2 * size) == col_ids // (2 * size))
                & (row_ids % (2 * size) >= size)
                & (col_ids % (2 * size) < size)
            )
            level_ref[level] = jnp.where(picked, 1.0, 0.0).astype(bf16)
            size *= 2
        for place in range(BASE - 1):
            chosen = jnp.where(row_ids == (col_ids // BASE) * BASE + place, 1.0, 0.0).astype(bf16)
            pick_ref[:, place * HALF : (place + 1) * HALF] = above(chosen, chosen)
        tri_rows, tri_cols = iotas((SPAN, SPAN))
        tri_ref[...] = jnp.where(tri_rows <= tri_cols, 1.0, 0.0).astype(bf16)

    def advance(head):
        maps = map_ref[head]
        high, low = run_ref[head, 0], run_ref[head, 1]
        moved = dot(maps, above(high, high)) + dot(maps[:, :DK], low)
        return beside(moved[:, :DV] + add_ref[head], moved[:, DV:])

    for head in range(heads):
        high, low = split(advance(head))
        run_ref[head, 0] = high
        run_ref[head, 1] = low
        start_out[0, head, 0] = high
        start_out[0, head, 1] = low

    gates = gate_ref[...]
    is_log = lax.broadcasted_iota(jnp.int32, gates.shape, 0) < heads
    logs = jnp.where(is_log, gates, 0.0)
    logs = above(logs, logs)
    high = logs.astype(bf16)
    rest = logs - high.astype(f32)
    mid = rest.astype(bf16)
    low = (rest - mid.astype(f32)).astype(bf16)
    tri = tri_ref[...]
    cum = (dot(high, tri) + dot(mid, tri) + dot(low, tri))[: gates.shape[0]]
    row_out[...] = cum
    packed = above(
        jnp.where(is_log, cum, gates),
        jnp.exp(cum),
        jnp.zeros((HALF - 2 * gates.shape[0], SPAN), f32),
    )
    cols = packed.T
    col_out[...] = cols

    first = step == 0
    key_feat = conv_silu(key_halo, key_prev, key_ref, key_taps, first)
    val_feat = conv_silu(val_halo, val_prev, val_ref, val_taps, first)

    keys, keys_t, grams = [], [], []
    for key_head in range(key_heads):
        feat = key_feat[:, key_head * DK : (key_head + 1) * DK]
        keyed = feat * lax.rsqrt(jnp.sum(feat * feat, axis=1, keepdims=True) + 1e-6)
        turned = keyed.T
        parts = split(turned)
        keyt_out[0, key_head, 0] = parts[0]
        keyt_out[0, key_head, 1] = parts[1]
        keys.append(keyed)
        keys_t.append(turned)
        grams.append(product(split(keyed), parts))

    diag, below = [], []
    for head in range(heads):
        gram = grams[head // group]
        beta_col = cols[:, heads + head : heads + head + 1]
        top, low, end = decay_blocks(cols[:, head : head + 1], cum[head : head + 1], True)
        diag.append(gram[:HALF, :HALF] * top * beta_col[:HALF])
        below.append(split(gram[HALF:, :HALF] * low * beta_col[HALF:]))
        diag.append(gram[HALF:, HALF:] * end * beta_col[HALF:])

    blocks = HALF // BASE
    compact = above(
        *(jnp.sum(jnp.where(base_mask, item, 0.0).reshape(blocks, BASE, HALF), axis=0) for item in diag)
    )
    spread = dot(beside(*split(compact)), pick_ref[...])
    count = len(diag)
    within = lax.broadcasted_iota(jnp.int32, (count, BASE, HALF), 1)
    lanes = lax.broadcasted_iota(jnp.int32, (count, BASE, HALF), 2)
    small = jnp.where(within == lanes % BASE, 1.0, 0.0).astype(f32)
    for place in range(BASE - 1):
        factor = spread[:, place * HALF : (place + 1) * HALF].reshape(count, BASE, HALF)
        small = small - factor * small[:, place : place + 1, :]
    inverses = [
        jnp.where(base_mask, jnp.broadcast_to(small[item][None], (blocks, BASE, HALF)).reshape(HALF, HALF), 0.0)
        for item in range(count)
    ]
    diag_parts = [split(item) for item in diag]
    size = BASE
    inv_parts = [split(item) for item in inverses]
    for level in range(level_ref.shape[0]):
        mask = odd_rows(level_ref[level], size)
        odd_parts = [tuple(odd_rows(part, size) for part in inv) for inv in inv_parts]
        inner = [
            product_small(tuple(odd_rows(part, size) * mask for part in item), inv)
            for item, inv in zip(diag_parts, inv_parts)
        ]
        fresh = [
            odd_rows(item, size) - product_small(odd, tuple(spread_rows(part, size) for part in split(part_in)))
            for item, odd, part_in in zip(inverses, odd_parts, inner)
        ]
        inv_parts = [
            tuple(merge_rows(old, new, size) for old, new in zip(inv, split(item)))
            for inv, item in zip(inv_parts, fresh)
        ]
        inverses = [merge_rows(old, new, size) for old, new in zip(inverses, fresh)]
        size *= 2

    right, tops, lows = [], [], []
    for head in range(heads):
        beta_col = cols[:, heads + head : heads + head + 1]
        exp_col = cols[:, 2 * heads + head : 2 * heads + head + 1]
        right.append(
            beside(keys[head // group] * (beta_col * exp_col), val_feat[:, head * DV : (head + 1) * DV] * beta_col)
        )
    for head in range(heads):
        tops.append(split(product(inv_parts[2 * head], split(right[head][:HALF]))))
    for head in range(heads):
        rest = right[head][HALF:] - product(below[head], tops[head])
        lows.append(split(product(inv_parts[2 * head + 1], split(rest))))
    for head in range(heads):
        solved = (above(tops[head][0], lows[head][0]), above(tops[head][1], lows[head][1]))
        solved_out[0, head, 0] = solved[0]
        solved_out[0, head, 1] = solved[1]
        cum_row = cum[head : head + 1]
        last = cum_row[:, SPAN - 1 : SPAN]
        faded = split(keys_t[head // group] * jnp.exp(last - cum_row))
        gathered = product(faded, solved)
        maps = unit * jnp.exp(last) - gathered[:, :DK]
        map_ref[head] = beside(*split(maps))
        add_ref[head] = gathered[:, DK:]

    @pl.when(step == pl.num_programs(0) - 1)
    def _():
        for head in range(heads):
            fin_ref[head] = advance(head)
        turn = turn_ref[0]
        for place, end_ref in enumerate((end0, end1, end2, end3)):
            end_ref[...] = fin_ref[lax.rem(turn + place, heads)]


def query_kernel(
    query_ref, query_prev, query_halo, taps_ref, keyt_ref, solved_ref, start_ref, row_ref, col_ref, *rest
):
    local_out, carry_out = rest[-3:-1]
    offset = rest[-1]
    first = pl.program_id(0) + offset == 0
    feat = conv_silu(query_halo, query_prev, query_ref, taps_ref, first)
    key_heads = query_ref.shape[1] // DK
    heads = solved_ref.shape[1]
    group = heads // key_heads
    queries, grams = [], []
    for key_head in range(key_heads):
        query = feat[:, key_head * DK : (key_head + 1) * DK]
        queries.append(query)
        grams.append(product(split(query), (keyt_ref[0, key_head, 0], keyt_ref[0, key_head, 1])))
    lifted = []
    for head in range(heads):
        gram = grams[head // group]
        top, low, end = decay_blocks(col_ref[:, head : head + 1], row_ref[head : head + 1], False)
        high, fine = solved_ref[0, head, 0], solved_ref[0, head, 1]
        upper = product(split(gram[:HALF, :HALF] * top), (high[:HALF], fine[:HALF]))
        wide = beside(gram[HALF:, :HALF] * low, gram[HALF:, HALF:] * end)
        lifted.append(above(upper, product(split(wide), (high, fine))))
    for head in range(heads):
        exp_col = col_ref[:, 2 * heads + head : 2 * heads + head + 1]
        reach = queries[head // group] * exp_col - lifted[head][:, :DK]
        seen = product(split(reach), (start_ref[0, head, 0], start_ref[0, head, 1]))
        local_out[:, head * DV : (head + 1) * DV] = seen[:, :DV] + lifted[head][:, DK:]
        carry_out[:, head * 2 * DK : (head + 1) * 2 * DK] = beside(*split(seen[:, DV:]))


def pack_kernel(query_ref, key_ref, val_ref, out_ref):
    out_ref[...] = beside(query_ref[...], key_ref[...], val_ref[...])


def compose_kernel(turn_ref, part0, part1, part2, part3, total_out, tail_out, prefix_out, all_ref):
    count = all_ref.shape[0]
    turn = turn_ref[0]
    for place, part in enumerate((part0, part1, part2, part3)):
        all_ref[lax.rem(turn + count - place, count)] = part[...]
    running = all_ref[0]
    prefix_out[0] = running
    for member in range(1, count):
        own = all_ref[member]
        moved = product(split(own[:, DV:]), split(running))
        running = beside(moved[:, :DV] + own[:, :DV], moved[:, DV:])
        if member < count - 1:
            prefix_out[member] = running
    total_out[...] = running
    tail_out[...] = running[:, :DV]


def enter_kernel(turn_ref, place_ref, near_ref, next_ref, far_ref, prefix_ref, out0, out1, out2, out3, all_ref):
    count = all_ref.shape[0]
    turn = turn_ref[0]
    place = place_ref[0]
    near, following, far = (
        jnp.where(place >= back, ref[...], 0.0)
        for back, ref in ((1, near_ref), (2, next_ref), (3, far_ref))
    )
    far = following[:, :DV] + product_small(split(following[:, DV:]), split(far))
    entry = near[:, :DV] + product_small(split(near[:, DV:]), split(far))
    parts = split(entry)
    all_ref[0] = entry
    for member in range(1, count):
        prefix = prefix_ref[member - 1]
        all_ref[member] = prefix[:, :DV] + product_small(split(prefix[:, DV:]), parts)
    for place, out in enumerate((out0, out1, out2, out3)):
        out[...] = all_ref[lax.rem(turn + place, count)]


def close_kernel(turn_ref, part0, part1, part2, part3, local_ref, carry_ref, gain_ref, out_ref, state_ref):
    heads = state_ref.shape[0]
    turn = turn_ref[0]

    @pl.when(pl.program_id(0) == 0)
    def _():
        for place, part in enumerate((part0, part1, part2, part3)):
            pair = beside(*split(part[...]))
            state_ref[lax.rem(turn + heads - place, heads)] = above(pair, pair)

    for head in range(heads):
        both = dot(carry_ref[:, head * 2 * DK : (head + 1) * 2 * DK], state_ref[head])
        value = local_ref[:, head * DV : (head + 1) * DV] + both[:, :DV] + both[:, DV:]
        scale = lax.rsqrt(jnp.sum(value * value, axis=1, keepdims=True) * (1.0 / DV) + 1e-6)
        gain = gain_ref[:, head * DV : (head + 1) * DV]
        out_ref[:, head * DV : (head + 1) * DV] = (value * scale * gain).astype(bf16)


def whole(shape):
    return pl.BlockSpec(shape, lambda *_: (0,) * len(shape))


def params(mebibytes):
    return pltpu.CompilerParams(dimension_semantics=("arbitrary",), vmem_limit_bytes=mebibytes * MIB)


def cost(flops, size, exps=0):
    return pl.CostEstimate(flops=flops, bytes_accessed=size, transcendentals=exps)


def per_device(
    query_in, key_in, value_in, log_decay, beta_gate, conv_query, conv_key, conv_value, norm_gain
):
    tok_rows, query_width = query_in.shape
    value_width = value_in.shape[1]
    key_heads = query_width // DK
    heads = value_width // DV
    spans = tok_rows // SPAN
    turn = lax.axis_index("outer").astype(jnp.int32).reshape(1)
    place = lax.axis_index("inner").astype(jnp.int32).reshape(1)
    query_far, key_in, value_in = (
        pltpu.with_memory_space_constraint(array, pltpu.HBM) for array in (query_in, key_in, value_in)
    )
    tail_block = tok_rows // 16 - 1
    all_width = 2 * query_width + value_width
    tails = pl.pallas_call(
        pack_kernel,
        grid=(1,),
        in_specs=[
            pl.BlockSpec((16, query_width), lambda i: (tail_block, 0)),
            pl.BlockSpec((16, query_width), lambda i: (tail_block, 0)),
            pl.BlockSpec((16, value_width), lambda i: (tail_block, 0)),
        ],
        out_specs=whole((16, all_width)),
        out_shape=jax.ShapeDtypeStruct((16, all_width), bf16),
        compiler_params=params(4),
        cost_estimate=cost(0, 64_000),
        name="pack",
    )(query_far, key_in, value_in)
    before = shifted(tails, ("inner", "outer"), 1, False)
    query_halo = pl.BlockSpec((16, query_width), lambda *_: (0, 0))
    key_halo = pl.BlockSpec((16, query_width), lambda *_: (0, 1))
    value_halo = pl.BlockSpec((16, value_width), lambda *_: (0, 2 * query_width // value_width))
    gates = above(log_decay.T, beta_gate.T)

    def prev_rows(offset):
        return lambda i, *_: (jnp.maximum((i + offset) * (SPAN // 16) - 1, 0), 0)

    square = jax.ShapeDtypeStruct((DK, 2 * DV), f32)
    keyt, solved, starts, rows, cols, *ends = pl.pallas_call(
        state_kernel,
        grid_spec=pltpu.PrefetchScalarGridSpec(
            num_scalar_prefetch=1,
            grid=(spans,),
            in_specs=[
                pl.BlockSpec((SPAN, query_width), lambda i, *_: (i, 0)),
                pl.BlockSpec((16, query_width), prev_rows(0)),
                key_halo,
                pl.BlockSpec((SPAN, value_width), lambda i, *_: (i, 0)),
                pl.BlockSpec((16, value_width), prev_rows(0)),
                value_halo,
                pl.BlockSpec((2 * heads, SPAN), lambda i, *_: (0, i)),
                whole((CONV, query_width)),
                whole((CONV, value_width)),
            ],
            out_specs=[
                pl.BlockSpec((1, key_heads, 2, DK, SPAN), lambda i, *_: (i, 0, 0, 0, 0)),
                pl.BlockSpec((1, heads, 2, SPAN, 2 * DV), lambda i, *_: (i, 0, 0, 0, 0)),
                pl.BlockSpec((1, heads, 2, DK, 2 * DV), lambda i, *_: (i, 0, 0, 0, 0)),
                pl.BlockSpec((2 * heads, SPAN), lambda i, *_: (0, i)),
                pl.BlockSpec((SPAN, HALF), lambda i, *_: (i, 0)),
            ]
            + [whole((DK, 2 * DV))] * 4,
            scratch_shapes=[
                pltpu.VMEM((heads, 2, DK, 2 * DV), bf16),
                pltpu.VMEM((heads, DK, 2 * DK), bf16),
                pltpu.VMEM((heads, DK, DV), f32),
                pltpu.VMEM((heads, DK, 2 * DV), f32),
                pltpu.VMEM((3, HALF, HALF), bf16),
                pltpu.VMEM((2 * HALF, (BASE - 1) * HALF), bf16),
                pltpu.VMEM((SPAN, SPAN), bf16),
            ],
        ),
        out_shape=[
            jax.ShapeDtypeStruct((spans, key_heads, 2, DK, SPAN), bf16),
            jax.ShapeDtypeStruct((spans, heads, 2, SPAN, 2 * DV), bf16),
            jax.ShapeDtypeStruct((spans, heads, 2, DK, 2 * DV), bf16),
            jax.ShapeDtypeStruct((2 * heads, tok_rows), f32),
            jax.ShapeDtypeStruct((tok_rows, HALF), f32),
        ]
        + [square] * 4,
        compiler_params=params(STATE_MIB),
        cost_estimate=cost(20_000_000_000, 20_000_000),
        name="state_path",
    )(turn, key_in, key_in, before, value_in, value_in, before, gates, conv_key, conv_value)

    parts = [ends[0]] + [shifted(ends[k], "outer", k, True) for k in (1, 2, 3)]

    out_types = (
        jax.ShapeDtypeStruct((tok_rows, value_width), f32),
        jax.ShapeDtypeStruct((tok_rows, 2 * value_width), bf16),
    )

    def query_part(offset, count, earlier):
        def body(*refs):
            query_kernel(*refs, offset)

        def at(i):
            return i + offset

        return pl.pallas_call(
            body,
            grid=(count,),
            in_specs=[
                pl.BlockSpec((SPAN, query_width), lambda i: (at(i), 0)),
                pl.BlockSpec((16, query_width), prev_rows(offset)),
                query_halo,
                whole((CONV, query_width)),
                pl.BlockSpec((1, key_heads, 2, DK, SPAN), lambda i: (at(i), 0, 0, 0, 0)),
                pl.BlockSpec((1, heads, 2, SPAN, 2 * DV), lambda i: (at(i), 0, 0, 0, 0)),
                pl.BlockSpec((1, heads, 2, DK, 2 * DV), lambda i: (at(i), 0, 0, 0, 0)),
                pl.BlockSpec((2 * heads, SPAN), lambda i: (0, at(i))),
                pl.BlockSpec((SPAN, HALF), lambda i: (at(i), 0)),
            ]
            + [pl.BlockSpec(memory_space=pl.ANY)] * len(earlier),
            out_specs=[
                pl.BlockSpec((SPAN, value_width), lambda i: (at(i), 0)),
                pl.BlockSpec((SPAN, 2 * value_width), lambda i: (at(i), 0)),
            ],
            out_shape=out_types,
            input_output_aliases={9 + k: k for k in range(len(earlier))},
            compiler_params=params(14),
            cost_estimate=cost(2_000_000_000 * count, 3_000_000 * count),
            name="query_path",
        )(query_in, query_in, before, conv_query, keyt, solved, starts, rows, cols, *earlier)

    cuts = (0, (3 * spans) // 8, (6 * spans) // 8, spans)
    seen = query_part(cuts[0], cuts[1] - cuts[0], ())
    parts, seen = lax.optimization_barrier((parts, seen))

    total, tail, prefix = pl.pallas_call(
        compose_kernel,
        grid_spec=pltpu.PrefetchScalarGridSpec(
            num_scalar_prefetch=1,
            grid=(1,),
            in_specs=[whole((DK, 2 * DV))] * 4,
            out_specs=[whole((DK, 2 * DV)), whole((DK, DV)), whole((3, DK, 2 * DV))],
            scratch_shapes=[pltpu.VMEM((4, DK, 2 * DV), f32)],
        ),
        out_shape=[
            square,
            jax.ShapeDtypeStruct((DK, DV), f32),
            jax.ShapeDtypeStruct((3, DK, 2 * DV), f32),
        ],
        compiler_params=params(8),
        cost_estimate=cost(100_000_000, 1_000_000),
        name="compose",
    )(turn, *parts)
    near = shifted(total, "inner", 1, True)
    middle = shifted(total, "inner", 2, True)
    far = shifted(tail, "inner", 3, True)

    seen = query_part(cuts[1], cuts[2] - cuts[1], seen)
    near, seen = lax.optimization_barrier((near, seen))
    local, carry = query_part(cuts[2], cuts[3] - cuts[2], seen)

    entries = pl.pallas_call(
        enter_kernel,
        grid_spec=pltpu.PrefetchScalarGridSpec(
            num_scalar_prefetch=2,
            grid=(1,),
            in_specs=[whole((DK, 2 * DV)), whole((DK, 2 * DV)), whole((DK, DV)), whole((3, DK, 2 * DV))],
            out_specs=[whole((DK, DV))] * 4,
            scratch_shapes=[pltpu.VMEM((4, DK, DV), f32)],
        ),
        out_shape=[jax.ShapeDtypeStruct((DK, DV), f32)] * 4,
        compiler_params=params(8),
        cost_estimate=cost(50_000_000, 1_000_000),
        name="enter",
    )(turn, place, near, middle, far, prefix)
    states = [entries[0]] + [shifted(entries[k], "outer", k, True) for k in (1, 2, 3)]

    return pl.pallas_call(
        close_kernel,
        grid_spec=pltpu.PrefetchScalarGridSpec(
            num_scalar_prefetch=1,
            grid=(spans,),
            in_specs=[whole((DK, DV))] * 4
            + [
                pl.BlockSpec((SPAN, value_width), lambda i, *_: (i, 0)),
                pl.BlockSpec((SPAN, 2 * value_width), lambda i, *_: (i, 0)),
                whole((1, value_width)),
            ],
            out_specs=pl.BlockSpec((SPAN, value_width), lambda i, *_: (i, 0)),
            scratch_shapes=[pltpu.VMEM((heads, 2 * DK, 2 * DV), bf16)],
        ),
        out_shape=jax.ShapeDtypeStruct((tok_rows, value_width), bf16),
        compiler_params=params(10),
        cost_estimate=cost(2_000_000_000, 10_000_000),
        name="close",
    )(turn, *states, local, carry, norm_gain.reshape(1, value_width))


def solution(mesh):
    in_specs = (
        P(("inner", "outer"), "head"),
        P(("inner", "outer"), "head"),
        P(("inner", "outer"), "head"),
        P(("inner", "outer"), "head"),
        P(("inner", "outer"), "head"),
        P(None, "head"),
        P(None, "head"),
        P(None, "head"),
        P("head"),
    )
    out_specs = P(("inner", "outer"), "head")
    return jax.shard_map(
        per_device, mesh=mesh, in_specs=in_specs, out_specs=out_specs, check_vma=False
    )
```

```python
import jax
import jax.numpy as jnp
from jax import lax
from jax.experimental import pallas as pl
from jax.experimental.pallas import tpu as pltpu
from jax.sharding import PartitionSpec as P

DK = 128
DV = 128
CONV = 4
SPAN = 256
HALF = 128
BASE = 16
MIB = 1024 * 1024
STATE_MIB = 16
QUERY_MIB = 14

f32 = jnp.float32
bf16 = jnp.bfloat16


def shifted(value, axis, steps, wrap):
    count = lax.axis_size(axis)
    if wrap:
        pairs = [(source, (source + steps) % count) for source in range(count)]
    else:
        pairs = [(source, source + steps) for source in range(count - steps)]
    return lax.ppermute(value, axis, pairs)


def split(value):
    high = value.astype(bf16)
    return high, (value - high.astype(f32)).astype(bf16)


def dot(left, right):
    return jnp.dot(left, right, preferred_element_type=f32)


def beside(*parts):
    return jnp.concatenate(parts, axis=1)


def above(*parts):
    return jnp.concatenate(parts, axis=0)


def product(left, right):
    if left[0].shape[1] == HALF:
        return dot(beside(*left), above(right[0], right[0])) + dot(left[0], right[1])
    return dot(left[0], right[0]) + dot(left[1], right[0]) + dot(left[0], right[1])


def product_small(left, right):
    return dot(beside(*left), above(right[0], right[0])) + dot(left[0], right[1])


def odd_rows(value, size):
    return above(*(value[start : start + size] for start in range(size, value.shape[0], 2 * size)))


def spread_rows(value, size):
    gap = jnp.zeros((size, value.shape[1]), value.dtype)
    return above(*(part for start in range(0, value.shape[0], size) for part in (gap, value[start : start + size])))


def merge_rows(value, odd, size):
    return above(
        *(
            part
            for start in range(0, odd.shape[0], size)
            for part in (value[2 * start : 2 * start + size], odd[start : start + size])
        )
    )


def iotas(shape):
    return lax.broadcasted_iota(jnp.int32, shape, 0), lax.broadcasted_iota(jnp.int32, shape, 1)


def conv_silu(halo, prev, cur, taps, first):
    prev = jnp.where(first, halo.astype(f32), prev.astype(f32))
    cur = cur.astype(f32)
    taps = taps.astype(f32)
    extended = above(prev[8:], cur)
    rows = cur.shape[0]
    total = taps[CONV - 1 : CONV] * cur
    for tap in range(CONV - 1):
        start = 8 - (CONV - 1) + tap
        total = total + taps[tap : tap + 1] * extended[start : start + rows]
    return total / (1.0 + jnp.exp(-total))


def decay_blocks(cum_col, cum_row, strict):
    row_ids, col_ids = iotas((HALF, HALF))
    keep = (row_ids > col_ids) if strict else (row_ids >= col_ids)
    top = jnp.exp(jnp.where(keep, cum_col[:HALF] - cum_row[:, :HALF], -1e30))
    low = jnp.exp(cum_col[HALF:] - cum_row[:, :HALF])
    end = jnp.exp(jnp.where(keep, cum_col[HALF:] - cum_row[:, HALF:], -1e30))
    return top, low, end


def state_kernel(
    turn_ref, halo_ref, key_ref, val_ref, gate_ref, key_taps, val_taps,
    keyt_out, solved_out, start_out, row_out, col_out, end0, end1, end2, end3,
    run_ref, map_ref, add_ref, fin_ref, level_ref, pick_ref, tri_ref,
    inv_ref, below_ref, keyed_ref, turned_ref, feat_ref, held_ref, cum_ref,
):
    heads = run_ref.shape[0]
    width = key_ref.shape[1]
    key_heads = width // DK
    spans = key_ref.shape[0] // SPAN
    halo = halo_ref[...]
    group = heads // key_heads
    row_ids, col_ids = iotas((HALF, HALF))
    unit = jnp.where(row_ids == col_ids, 1.0, 0.0).astype(f32)
    base_mask = (row_ids // BASE) == (col_ids // BASE)

    zeros = jnp.zeros((HALF, HALF), f32)
    for head in range(heads):
        run_ref[head, 0] = beside(zeros, unit).astype(bf16)
        run_ref[head, 1] = beside(zeros, zeros).astype(bf16)
        map_ref[head] = beside(unit, zeros).astype(bf16)
        add_ref[head] = zeros
    size = BASE
    for level in range(level_ref.shape[0]):
        picked = (
            (row_ids // (2 * size) == col_ids // (2 * size))
            & (row_ids % (2 * size) >= size)
            & (col_ids % (2 * size) < size)
        )
        level_ref[level] = jnp.where(picked, 1.0, 0.0).astype(bf16)
        size *= 2
    for place in range(BASE - 1):
        chosen = jnp.where(row_ids == (col_ids // BASE) * BASE + place, 1.0, 0.0).astype(bf16)
        pick_ref[:, place * HALF : (place + 1) * HALF] = above(chosen, chosen)
    tri_rows, tri_cols = iotas((SPAN, SPAN))
    tri_ref[...] = jnp.where(tri_rows <= tri_cols, 1.0, 0.0).astype(bf16)
    for ref in (inv_ref, below_ref, keyed_ref, turned_ref, feat_ref, held_ref, cum_ref):
        ref[...] = jnp.zeros(ref.shape, ref.dtype)

    def advance(head):
        maps = map_ref[head]
        high, low = run_ref[head, 0], run_ref[head, 1]
        moved = dot(maps, above(high, high)) + dot(maps[:, :DK], low)
        return beside(moved[:, :DV] + add_ref[head], moved[:, DV:])

    def follow(span):
        for head in range(heads):
            high, low = split(advance(head))
            run_ref[head, 0] = high
            run_ref[head, 1] = low
            start_out[span, head, 0] = high
            start_out[span, head, 1] = low

    def prepare(span):
        rows_at = pl.multiple_of(span * SPAN, SPAN)
        here = pl.ds(rows_at, SPAN)
        ahead = pl.ds(pl.multiple_of(jnp.maximum(rows_at - 16, 0), 16), 16)
        gates = gate_ref[:, here]
        is_log = lax.broadcasted_iota(jnp.int32, gates.shape, 0) < heads
        logs = jnp.where(is_log, gates, 0.0)
        logs = above(logs, logs)
        high = logs.astype(bf16)
        rest = logs - high.astype(f32)
        mid = rest.astype(bf16)
        low = (rest - mid.astype(f32)).astype(bf16)
        tri = tri_ref[...]
        cum = (dot(high, tri) + dot(mid, tri) + dot(low, tri))[: gates.shape[0]]
        row_out[:, here] = cum
        packed = above(
            jnp.where(is_log, cum, gates),
            jnp.exp(cum),
            jnp.zeros((HALF - 2 * gates.shape[0], SPAN), f32),
        )
        cols = packed.T
        col_out[here, :] = cols

        first = span == 0
        key_feat = conv_silu(halo[:, width : 2 * width], key_ref[ahead, :], key_ref[here, :], key_taps[...], first)
        val_feat = conv_silu(halo[:, 2 * width :], val_ref[ahead, :], val_ref[here, :], val_taps[...], first)

        keys, keys_t, grams = [], [], []
        for key_head in range(key_heads):
            feat = key_feat[:, key_head * DK : (key_head + 1) * DK]
            keyed = feat * lax.rsqrt(jnp.sum(feat * feat, axis=1, keepdims=True) + 1e-6)
            turned = keyed.T
            parts = split(turned)
            keyt_out[span, key_head, 0] = parts[0]
            keyt_out[span, key_head, 1] = parts[1]
            keys.append(keyed)
            keys_t.append(turned)
            grams.append(product(split(keyed), parts))

        diag, below = [], []
        for head in range(heads):
            gram = grams[head // group]
            beta_col = cols[:, heads + head : heads + head + 1]
            top, low, end = decay_blocks(cols[:, head : head + 1], cum[head : head + 1], True)
            diag.append(gram[:HALF, :HALF] * top * beta_col[:HALF])
            below.append(split(gram[HALF:, :HALF] * low * beta_col[HALF:]))
            diag.append(gram[HALF:, HALF:] * end * beta_col[HALF:])

        blocks = HALF // BASE
        compact = above(
            *(jnp.sum(jnp.where(base_mask, item, 0.0).reshape(blocks, BASE, HALF), axis=0) for item in diag)
        )
        spread = dot(beside(*split(compact)), pick_ref[...])
        count = len(diag)
        within = lax.broadcasted_iota(jnp.int32, (count, BASE, HALF), 1)
        lanes = lax.broadcasted_iota(jnp.int32, (count, BASE, HALF), 2)
        small = jnp.where(within == lanes % BASE, 1.0, 0.0).astype(f32)
        for place in range(BASE - 1):
            factor = spread[:, place * HALF : (place + 1) * HALF].reshape(count, BASE, HALF)
            small = small - factor * small[:, place : place + 1, :]
        inverses = [
            jnp.where(base_mask, jnp.broadcast_to(small[item][None], (blocks, BASE, HALF)).reshape(HALF, HALF), 0.0)
            for item in range(count)
        ]
        diag_parts = [split(item) for item in diag]
        size = BASE
        inv_parts = [split(item) for item in inverses]
        for level in range(level_ref.shape[0]):
            mask = odd_rows(level_ref[level], size)
            odd_parts = [tuple(odd_rows(part, size) for part in inv) for inv in inv_parts]
            inner = [
                product_small(tuple(odd_rows(part, size) * mask for part in item), inv)
                for item, inv in zip(diag_parts, inv_parts)
            ]
            fresh = [
                odd_rows(item, size) - product_small(odd, tuple(spread_rows(part, size) for part in split(part_in)))
                for item, odd, part_in in zip(inverses, odd_parts, inner)
            ]
            inv_parts = [
                tuple(merge_rows(old, new, size) for old, new in zip(inv, split(item)))
                for inv, item in zip(inv_parts, fresh)
            ]
            inverses = [merge_rows(old, new, size) for old, new in zip(inverses, fresh)]
            size *= 2

        for item in range(count):
            inv_ref[item, 0], inv_ref[item, 1] = inv_parts[item]
        for head in range(heads):
            below_ref[head, 0], below_ref[head, 1] = below[head]
        for key_head in range(key_heads):
            keyed_ref[key_head] = keys[key_head]
            turned_ref[key_head] = keys_t[key_head]
        feat_ref[...] = val_feat
        held_ref[...] = cols
        cum_ref[...] = cum

    def solve(span):
        inv_parts = [(inv_ref[item, 0], inv_ref[item, 1]) for item in range(2 * heads)]
        below = [(below_ref[head, 0], below_ref[head, 1]) for head in range(heads)]
        keys = [keyed_ref[key_head] for key_head in range(key_heads)]
        keys_t = [turned_ref[key_head] for key_head in range(key_heads)]
        val_feat, cols, cum = feat_ref[...], held_ref[...], cum_ref[...]
        right, tops, lows = [], [], []
        for head in range(heads):
            beta_col = cols[:, heads + head : heads + head + 1]
            exp_col = cols[:, 2 * heads + head : 2 * heads + head + 1]
            right.append(
                beside(keys[head // group] * (beta_col * exp_col), val_feat[:, head * DV : (head + 1) * DV] * beta_col)
            )
        for head in range(heads):
            tops.append(split(product(inv_parts[2 * head], split(right[head][:HALF]))))
        for head in range(heads):
            rest = right[head][HALF:] - product(below[head], tops[head])
            lows.append(split(product(inv_parts[2 * head + 1], split(rest))))
        for head in range(heads):
            solved = (above(tops[head][0], lows[head][0]), above(tops[head][1], lows[head][1]))
            solved_out[span, head, 0] = solved[0]
            solved_out[span, head, 1] = solved[1]
            cum_row = cum[head : head + 1]
            last = cum_row[:, SPAN - 1 : SPAN]
            faded = split(keys_t[head // group] * jnp.exp(last - cum_row))
            gathered = product(faded, solved)
            maps = unit * jnp.exp(last) - gathered[:, :DK]
            map_ref[head] = beside(*split(maps))
            add_ref[head] = gathered[:, DK:]

    def one_round(span, carried):
        before = jnp.maximum(span - 1, 0)
        follow(before)
        solve(before)
        prepare(span)
        return carried

    lax.fori_loop(0, spans, one_round, 0)
    follow(spans - 1)
    solve(spans - 1)
    for head in range(heads):
        fin_ref[head] = advance(head)
    turn = turn_ref[0]
    for place, end_ref in enumerate((end0, end1, end2, end3)):
        end_ref[...] = fin_ref[lax.rem(turn + place, heads)]


def query_kernel(
    query_ref, halo_ref, taps_ref, keyt_ref, solved_ref, start_ref, row_ref, col_ref, *rest
):
    local_out, carry_out, begin, finish = rest[-4:]
    width = query_ref.shape[1]
    key_heads = width // DK
    heads = solved_ref.shape[1]
    group = heads // key_heads
    halo = halo_ref[:, :width]

    def one_span(span, carried):
        here = pl.ds(span * SPAN, SPAN)
        ahead = pl.ds(max(span * SPAN - 16, 0), 16)
        feat = conv_silu(halo, query_ref[ahead, :], query_ref[here, :], taps_ref[...], span == 0)
        cum_rows = row_ref[:, here]
        cols = col_ref[here, :]
        queries, grams = [], []
        for key_head in range(key_heads):
            query = feat[:, key_head * DK : (key_head + 1) * DK]
            queries.append(query)
            grams.append(product(split(query), (keyt_ref[span, key_head, 0], keyt_ref[span, key_head, 1])))
        lifted = []
        for head in range(heads):
            gram = grams[head // group]
            top, low, end = decay_blocks(cols[:, head : head + 1], cum_rows[head : head + 1], False)
            high, fine = solved_ref[span, head, 0], solved_ref[span, head, 1]
            upper = product(split(gram[:HALF, :HALF] * top), (high[:HALF], fine[:HALF]))
            wide = beside(gram[HALF:, :HALF] * low, gram[HALF:, HALF:] * end)
            lifted.append(above(upper, product(split(wide), (high, fine))))
        for head in range(heads):
            exp_col = cols[:, 2 * heads + head : 2 * heads + head + 1]
            reach = queries[head // group] * exp_col - lifted[head][:, :DK]
            seen = product(split(reach), (start_ref[span, head, 0], start_ref[span, head, 1]))
            local_out[here, head * DV : (head + 1) * DV] = seen[:, :DV] + lifted[head][:, DK:]
            carry_out[here, head * 2 * DK : (head + 1) * 2 * DK] = beside(*split(seen[:, DV:]))
        return carried

    for span in range(begin, finish):
        one_span(span, 0)


def pack_kernel(query_ref, key_ref, val_ref, out_ref):
    out_ref[...] = beside(query_ref[...], key_ref[...], val_ref[...])


def compose_kernel(turn_ref, part0, part1, part2, part3, total_out, tail_out, prefix_out, all_ref):
    count = all_ref.shape[0]
    turn = turn_ref[0]
    for place, part in enumerate((part0, part1, part2, part3)):
        all_ref[lax.rem(turn + count - place, count)] = part[...]
    running = all_ref[0]
    prefix_out[0] = running
    for member in range(1, count):
        own = all_ref[member]
        moved = product(split(own[:, DV:]), split(running))
        running = beside(moved[:, :DV] + own[:, :DV], moved[:, DV:])
        if member < count - 1:
            prefix_out[member] = running
    total_out[...] = running
    tail_out[...] = running[:, :DV]


def enter_kernel(turn_ref, place_ref, near_ref, next_ref, far_ref, prefix_ref, out0, out1, out2, out3, all_ref):
    count = all_ref.shape[0]
    turn = turn_ref[0]
    place = place_ref[0]
    near, following, far = (
        jnp.where(place >= back, ref[...], 0.0)
        for back, ref in ((1, near_ref), (2, next_ref), (3, far_ref))
    )
    far = following[:, :DV] + product_small(split(following[:, DV:]), split(far))
    entry = near[:, :DV] + product_small(split(near[:, DV:]), split(far))
    parts = split(entry)
    all_ref[0] = entry
    for member in range(1, count):
        prefix = prefix_ref[member - 1]
        all_ref[member] = prefix[:, :DV] + product_small(split(prefix[:, DV:]), parts)
    for place, out in enumerate((out0, out1, out2, out3)):
        out[...] = all_ref[lax.rem(turn + place, count)]


def close_kernel(
    turn_ref, part0, part1, part2, part3, local_ref, carry_ref, gain_ref, out_ref, state_ref, done_ref, sems
):
    heads = state_ref.shape[0]
    turn = turn_ref[0]
    for place, part in enumerate((part0, part1, part2, part3)):
        pair = beside(*split(part[...]))
        state_ref[lax.rem(turn + heads - place, heads)] = above(pair, pair)
    spans = local_ref.shape[0] // SPAN

    def copy_out(span):
        here = pl.ds(span * SPAN, SPAN)
        return pltpu.make_async_copy(done_ref.at[here, :], out_ref.at[here, :], sems.at[span])

    def one_span(span, carried):
        here = pl.ds(span * SPAN, SPAN)
        for head in range(heads):
            both = dot(carry_ref[here, head * 2 * DK : (head + 1) * 2 * DK], state_ref[head])
            value = local_ref[here, head * DV : (head + 1) * DV] + both[:, :DV] + both[:, DV:]
            scale = lax.rsqrt(jnp.sum(value * value, axis=1, keepdims=True) * (1.0 / DV) + 1e-6)
            gain = gain_ref[:, head * DV : (head + 1) * DV]
            done_ref[here, head * DV : (head + 1) * DV] = (value * scale * gain).astype(bf16)
        copy_out(span).start()
        return carried

    def finish(span, carried):
        copy_out(span).wait()
        return carried

    for span in range(spans):
        one_span(span, 0)
    for span in range(spans):
        finish(span, 0)


def whole(shape):
    return pl.BlockSpec(shape, lambda *_: (0,) * len(shape))


def params(mebibytes):
    return pltpu.CompilerParams(dimension_semantics=("arbitrary",), vmem_limit_bytes=mebibytes * MIB)


def cost(flops, size, exps=0):
    return pl.CostEstimate(flops=flops, bytes_accessed=size, transcendentals=exps)


def per_device(
    query_in, key_in, value_in, log_decay, beta_gate, conv_query, conv_key, conv_value, norm_gain
):
    tok_rows, query_width = query_in.shape
    value_width = value_in.shape[1]
    key_heads = query_width // DK
    heads = value_width // DV
    spans = tok_rows // SPAN
    turn = lax.axis_index("outer").astype(jnp.int32).reshape(1)
    place = lax.axis_index("inner").astype(jnp.int32).reshape(1)
    far_in = tuple(
        pltpu.with_memory_space_constraint(array, pltpu.HBM) for array in (query_in, key_in, value_in)
    )
    tail_block = tok_rows // 16 - 1
    all_width = 2 * query_width + value_width
    tails = pl.pallas_call(
        pack_kernel,
        grid=(1,),
        in_specs=[
            pl.BlockSpec((16, query_width), lambda i: (tail_block, 0)),
            pl.BlockSpec((16, query_width), lambda i: (tail_block, 0)),
            pl.BlockSpec((16, value_width), lambda i: (tail_block, 0)),
        ],
        out_specs=whole((16, all_width)),
        out_shape=jax.ShapeDtypeStruct((16, all_width), bf16),
        compiler_params=params(4),
        cost_estimate=cost(0, 64_000),
        name="pack",
    )(*far_in)
    before = shifted(tails, ("inner", "outer"), 1, False)
    gates = above(log_decay.T, beta_gate.T)

    square = jax.ShapeDtypeStruct((DK, 2 * DV), f32)
    keyt, solved, starts, rows, cols, *ends = pl.pallas_call(
        state_kernel,
        grid_spec=pltpu.PrefetchScalarGridSpec(
            num_scalar_prefetch=1,
            grid=(),
            in_specs=[pl.BlockSpec(memory_space=pltpu.VMEM)] * 6,
            out_specs=[pl.BlockSpec(memory_space=pltpu.VMEM)] * 9,
            scratch_shapes=[
                pltpu.VMEM((heads, 2, DK, 2 * DV), bf16),
                pltpu.VMEM((heads, DK, 2 * DK), bf16),
                pltpu.VMEM((heads, DK, DV), f32),
                pltpu.VMEM((heads, DK, 2 * DV), f32),
                pltpu.VMEM((3, HALF, HALF), bf16),
                pltpu.VMEM((2 * HALF, (BASE - 1) * HALF), bf16),
                pltpu.VMEM((SPAN, SPAN), bf16),
                pltpu.VMEM((2 * heads, 2, HALF, HALF), bf16),
                pltpu.VMEM((heads, 2, HALF, HALF), bf16),
                pltpu.VMEM((key_heads, SPAN, DK), f32),
                pltpu.VMEM((key_heads, DK, SPAN), f32),
                pltpu.VMEM((SPAN, value_width), f32),
                pltpu.VMEM((SPAN, HALF), f32),
                pltpu.VMEM((2 * heads, SPAN), f32),
            ],
        ),
        out_shape=[
            jax.ShapeDtypeStruct((spans, key_heads, 2, DK, SPAN), bf16),
            jax.ShapeDtypeStruct((spans, heads, 2, SPAN, 2 * DV), bf16),
            jax.ShapeDtypeStruct((spans, heads, 2, DK, 2 * DV), bf16),
            jax.ShapeDtypeStruct((2 * heads, tok_rows), f32),
            jax.ShapeDtypeStruct((tok_rows, HALF), f32),
        ]
        + [square] * 4,
        compiler_params=pltpu.CompilerParams(vmem_limit_bytes=STATE_MIB * MIB),
        cost_estimate=cost(20_000_000_000, 20_000_000),
        name="state_path",
    )(turn, before, key_in, value_in, gates, conv_key, conv_value)

    parts = [ends[0]] + [shifted(ends[k], "outer", k, True) for k in (1, 2, 3)]

    out_types = (
        jax.ShapeDtypeStruct((tok_rows, value_width), f32),
        jax.ShapeDtypeStruct((tok_rows, 2 * value_width), bf16),
    )

    def query_part(offset, count, earlier):
        def body(*refs):
            query_kernel(*refs, offset, offset + count)

        return pl.pallas_call(
            body,
            in_specs=[pl.BlockSpec(memory_space=pltpu.VMEM)] * (8 + len(earlier)),
            out_specs=[pl.BlockSpec(memory_space=pltpu.VMEM)] * 2,
            out_shape=out_types,
            input_output_aliases={8 + k: k for k in range(len(earlier))},
            compiler_params=pltpu.CompilerParams(vmem_limit_bytes=QUERY_MIB * MIB),
            cost_estimate=cost(2_000_000_000 * count, 3_000_000 * count),
            name="query_path",
        )(query_in, before, conv_query, keyt, solved, starts, rows, cols, *earlier)

    cuts = (0, (3 * spans) // 8, (5 * spans) // 8, spans)
    seen = query_part(cuts[0], cuts[1] - cuts[0], ())
    parts, seen = lax.optimization_barrier((parts, seen))

    total, tail, prefix = pl.pallas_call(
        compose_kernel,
        grid_spec=pltpu.PrefetchScalarGridSpec(
            num_scalar_prefetch=1,
            grid=(1,),
            in_specs=[whole((DK, 2 * DV))] * 4,
            out_specs=[whole((DK, 2 * DV)), whole((DK, DV)), whole((3, DK, 2 * DV))],
            scratch_shapes=[pltpu.VMEM((4, DK, 2 * DV), f32)],
        ),
        out_shape=[
            square,
            jax.ShapeDtypeStruct((DK, DV), f32),
            jax.ShapeDtypeStruct((3, DK, 2 * DV), f32),
        ],
        compiler_params=params(8),
        cost_estimate=cost(100_000_000, 1_000_000),
        name="compose",
    )(turn, *parts)
    near = shifted(total, "inner", 1, True)
    middle = shifted(total, "inner", 2, True)
    far = shifted(tail, "inner", 3, True)

    seen = query_part(cuts[1], cuts[2] - cuts[1], seen)
    near, seen = lax.optimization_barrier((near, seen))
    local, carry = query_part(cuts[2], cuts[3] - cuts[2], seen)

    entries = pl.pallas_call(
        enter_kernel,
        grid_spec=pltpu.PrefetchScalarGridSpec(
            num_scalar_prefetch=2,
            grid=(1,),
            in_specs=[whole((DK, 2 * DV)), whole((DK, 2 * DV)), whole((DK, DV)), whole((3, DK, 2 * DV))],
            out_specs=[whole((DK, DV))] * 4,
            scratch_shapes=[pltpu.VMEM((4, DK, DV), f32)],
        ),
        out_shape=[jax.ShapeDtypeStruct((DK, DV), f32)] * 4,
        compiler_params=params(8),
        cost_estimate=cost(50_000_000, 1_000_000),
        name="enter",
    )(turn, place, near, middle, far, prefix)
    states = [entries[0]] + [shifted(entries[k], "outer", k, True) for k in (1, 2, 3)]

    return pl.pallas_call(
        close_kernel,
        grid_spec=pltpu.PrefetchScalarGridSpec(
            num_scalar_prefetch=1,
            grid=(),
            in_specs=[pl.BlockSpec(memory_space=pltpu.VMEM)] * 7,
            out_specs=pl.BlockSpec(memory_space=pltpu.HBM),
            scratch_shapes=[
                pltpu.VMEM((heads, 2 * DK, 2 * DV), bf16),
                pltpu.VMEM((tok_rows, value_width), bf16),
                pltpu.SemaphoreType.DMA((spans,)),
            ],
        ),
        out_shape=jax.ShapeDtypeStruct((tok_rows, value_width), bf16),
        compiler_params=pltpu.CompilerParams(vmem_limit_bytes=12 * MIB),
        cost_estimate=cost(2_000_000_000, 10_000_000),
        name="close",
    )(turn, *states, local, carry, norm_gain.reshape(1, value_width))


def solution(mesh):
    in_specs = (
        P(("inner", "outer"), "head"),
        P(("inner", "outer"), "head"),
        P(("inner", "outer"), "head"),
        P(("inner", "outer"), "head"),
        P(("inner", "outer"), "head"),
        P(None, "head"),
        P(None, "head"),
        P(None, "head"),
        P("head"),
    )
    out_specs = P(("inner", "outer"), "head")
    return jax.shard_map(
        per_device, mesh=mesh, in_specs=in_specs, out_specs=out_specs, check_vma=False
    )
```

```python
import jax
import jax.numpy as jnp
from jax import lax
from jax.experimental import pallas as pl
from jax.experimental.pallas import tpu as pltpu
from jax.sharding import PartitionSpec as P

DK = 128
DV = 128
CONV = 4
SPAN = 256
HALF = 128
BASE = 16
GROUP = 2
MIB = 1024 * 1024
STATE_MIB = 24
QUERY_MIB = 14

f32 = jnp.float32
bf16 = jnp.bfloat16


def shifted(value, axis, steps, wrap):
    count = lax.axis_size(axis)
    if wrap:
        pairs = [(source, (source + steps) % count) for source in range(count)]
    else:
        pairs = [(source, source + steps) for source in range(count - steps)]
    return lax.ppermute(value, axis, pairs)


def split(value):
    high = value.astype(bf16)
    return high, (value - high.astype(f32)).astype(bf16)


def dot(left, right):
    return jnp.dot(left, right, preferred_element_type=f32)


def beside(*parts):
    return jnp.concatenate(parts, axis=1)


def above(*parts):
    return jnp.concatenate(parts, axis=0)


def product(left, right):
    if left[0].shape[1] == HALF:
        return dot(beside(*left), above(right[0], right[0])) + dot(left[0], right[1])
    return dot(left[0], right[0]) + dot(left[1], right[0]) + dot(left[0], right[1])


def product_small(left, right):
    return dot(beside(*left), above(right[0], right[0])) + dot(left[0], right[1])


def odd_rows(value, size):
    return above(*(value[start : start + size] for start in range(size, value.shape[0], 2 * size)))


def spread_rows(value, size):
    gap = jnp.zeros((size, value.shape[1]), value.dtype)
    return above(*(part for start in range(0, value.shape[0], size) for part in (gap, value[start : start + size])))


def merge_rows(value, odd, size):
    return above(
        *(
            part
            for start in range(0, odd.shape[0], size)
            for part in (value[2 * start : 2 * start + size], odd[start : start + size])
        )
    )


def iotas(shape):
    return lax.broadcasted_iota(jnp.int32, shape, 0), lax.broadcasted_iota(jnp.int32, shape, 1)


def conv_silu(halo, prev, cur, taps, first):
    prev = jnp.where(first, halo.astype(f32), prev.astype(f32))
    cur = cur.astype(f32)
    taps = taps.astype(f32)
    extended = above(prev[8:], cur)
    rows = cur.shape[0]
    total = taps[CONV - 1 : CONV] * cur
    for tap in range(CONV - 1):
        start = 8 - (CONV - 1) + tap
        total = total + taps[tap : tap + 1] * extended[start : start + rows]
    return total / (1.0 + jnp.exp(-total))


def decay_blocks(cum_col, cum_row, strict):
    row_ids, col_ids = iotas((HALF, HALF))
    keep = (row_ids > col_ids) if strict else (row_ids >= col_ids)
    top = jnp.exp(jnp.where(keep, cum_col[:HALF] - cum_row[:, :HALF], -1e30))
    low = jnp.exp(cum_col[HALF:] - cum_row[:, :HALF])
    end = jnp.exp(jnp.where(keep, cum_col[HALF:] - cum_row[:, HALF:], -1e30))
    return top, low, end


def state_kernel(
    turn_ref, halo_ref, key_ref, val_ref, gate_ref, key_taps, val_taps,
    keyt_out, solved_out, start_out, row_out, col_out, end0, end1, end2, end3,
    run_ref, map_ref, add_ref, fin_ref, level_ref, pick_ref, tri_ref,
    inv_ref, below_ref, keyed_ref, turned_ref, feat_ref, held_ref, cum_ref,
):
    heads = run_ref.shape[0]
    width = key_ref.shape[1]
    key_heads = width // DK
    spans = key_ref.shape[0] // SPAN
    halo = halo_ref[...]
    group = heads // key_heads
    row_ids, col_ids = iotas((HALF, HALF))
    unit = jnp.where(row_ids == col_ids, 1.0, 0.0).astype(f32)
    base_mask = (row_ids // BASE) == (col_ids // BASE)

    zeros = jnp.zeros((HALF, HALF), f32)
    for head in range(heads):
        run_ref[head, 0] = beside(zeros, unit).astype(bf16)
        run_ref[head, 1] = beside(zeros, zeros).astype(bf16)
        for sub in range(GROUP):
            map_ref[sub, head] = beside(unit, zeros).astype(bf16)
            add_ref[sub, head] = zeros
    size = BASE
    for level in range(level_ref.shape[0]):
        picked = (
            (row_ids // (2 * size) == col_ids // (2 * size))
            & (row_ids % (2 * size) >= size)
            & (col_ids % (2 * size) < size)
        )
        level_ref[level] = jnp.where(picked, 1.0, 0.0).astype(bf16)
        size *= 2
    for place in range(BASE - 1):
        chosen = jnp.where(row_ids == (col_ids // BASE) * BASE + place, 1.0, 0.0).astype(bf16)
        pick_ref[:, place * HALF : (place + 1) * HALF] = above(chosen, chosen)
    tri_rows, tri_cols = iotas((SPAN, SPAN))
    tri_ref[...] = jnp.where(tri_rows <= tri_cols, 1.0, 0.0).astype(bf16)

    def advance(head, sub, high, low):
        maps = map_ref[sub, head]
        moved = dot(maps, above(high, high)) + dot(maps[:, :DK], low)
        return beside(moved[:, :DV] + add_ref[sub, head], moved[:, DV:])

    def follow(group_at):
        for head in range(heads):
            high, low = run_ref[head, 0], run_ref[head, 1]
            for sub in range(GROUP):
                start_out[group_at * GROUP + sub, head, 0] = high
                start_out[group_at * GROUP + sub, head, 1] = low
                reached = advance(head, sub, high, low)
                high, low = split(reached)
            run_ref[head, 0] = high
            run_ref[head, 1] = low
            fin_ref[head] = reached

    def prepare(group_at):
        feats = []
        for sub in range(GROUP):
            span = group_at * GROUP + sub
            rows_at = pl.multiple_of(span * SPAN, SPAN)
            here = pl.ds(rows_at, SPAN)
            ahead = pl.ds(pl.multiple_of(jnp.maximum(rows_at - 16, 0), 16), 16)
            gates = gate_ref[:, here]
            is_log = lax.broadcasted_iota(jnp.int32, gates.shape, 0) < heads
            logs = jnp.where(is_log, gates, 0.0)
            logs = above(logs, logs)
            high = logs.astype(bf16)
            rest = logs - high.astype(f32)
            mid = rest.astype(bf16)
            low = (rest - mid.astype(f32)).astype(bf16)
            tri = tri_ref[...]
            cum = (dot(high, tri) + dot(mid, tri) + dot(low, tri))[: gates.shape[0]]
            row_out[:, here] = cum
            packed = above(
                jnp.where(is_log, cum, gates),
                jnp.exp(cum),
                jnp.zeros((HALF - 2 * gates.shape[0], SPAN), f32),
            )
            cols = packed.T
            col_out[here, :] = cols
            first = span == 0
            key_feat = conv_silu(
                halo[:, width : 2 * width], key_ref[ahead, :], key_ref[here, :], key_taps[...], first
            )
            val_feat = conv_silu(
                halo[:, 2 * width :], val_ref[ahead, :], val_ref[here, :], val_taps[...], first
            )
            feats.append((span, cum, cols, key_feat, val_feat))

        diag, below, keyed_all = [], [], []
        for span, cum, cols, key_feat, _ in feats:
            grams = []
            for key_head in range(key_heads):
                feat = key_feat[:, key_head * DK : (key_head + 1) * DK]
                keyed = feat * lax.rsqrt(jnp.sum(feat * feat, axis=1, keepdims=True) + 1e-6)
                turned = keyed.T
                parts = split(turned)
                keyt_out[span, key_head, 0] = parts[0]
                keyt_out[span, key_head, 1] = parts[1]
                keyed_all.append((keyed, turned))
                grams.append(product(split(keyed), parts))
            for head in range(heads):
                gram = grams[head // group]
                beta_col = cols[:, heads + head : heads + head + 1]
                top, low, end = decay_blocks(cols[:, head : head + 1], cum[head : head + 1], True)
                diag.append(gram[:HALF, :HALF] * top * beta_col[:HALF])
                below.append(split(gram[HALF:, :HALF] * low * beta_col[HALF:]))
                diag.append(gram[HALF:, HALF:] * end * beta_col[HALF:])

        blocks = HALF // BASE
        compact = above(
            *(jnp.sum(jnp.where(base_mask, item, 0.0).reshape(blocks, BASE, HALF), axis=0) for item in diag)
        )
        spread = dot(beside(*split(compact)), pick_ref[...])
        count = len(diag)
        within = lax.broadcasted_iota(jnp.int32, (count, BASE, HALF), 1)
        lanes = lax.broadcasted_iota(jnp.int32, (count, BASE, HALF), 2)
        small = jnp.where(within == lanes % BASE, 1.0, 0.0).astype(f32)
        for place in range(BASE - 1):
            factor = spread[:, place * HALF : (place + 1) * HALF].reshape(count, BASE, HALF)
            small = small - factor * small[:, place : place + 1, :]
        inverses = [
            jnp.where(
                base_mask, jnp.broadcast_to(small[item][None], (blocks, BASE, HALF)).reshape(HALF, HALF), 0.0
            )
            for item in range(count)
        ]
        diag_parts = [split(item) for item in diag]
        size = BASE
        inv_parts = [split(item) for item in inverses]
        for level in range(level_ref.shape[0]):
            mask = odd_rows(level_ref[level], size)
            odd_parts = [tuple(odd_rows(part, size) for part in inv) for inv in inv_parts]
            inner = [
                product_small(tuple(odd_rows(part, size) * mask for part in item), inv)
                for item, inv in zip(diag_parts, inv_parts)
            ]
            fresh = [
                odd_rows(item, size) - product_small(odd, tuple(spread_rows(part, size) for part in split(part_in)))
                for item, odd, part_in in zip(inverses, odd_parts, inner)
            ]
            inv_parts = [
                tuple(merge_rows(old, new, size) for old, new in zip(inv, split(item)))
                for inv, item in zip(inv_parts, fresh)
            ]
            inverses = [merge_rows(old, new, size) for old, new in zip(inverses, fresh)]
            size *= 2

        for item in range(count):
            inv_ref[item, 0], inv_ref[item, 1] = inv_parts[item]
        for item, parts in enumerate(below):
            below_ref[item, 0], below_ref[item, 1] = parts
        for item, (keyed, turned) in enumerate(keyed_all):
            keyed_ref[item] = keyed
            turned_ref[item] = turned
        for sub, (_, cum, cols, _, val_feat) in enumerate(feats):
            feat_ref[sub] = val_feat
            held_ref[sub] = cols
            cum_ref[sub] = cum

    def solve(group_at):
        both = [(sub, head) for sub in range(GROUP) for head in range(heads)]
        tops, lows, right = [], [], []
        for sub, head in both:
            cols = held_ref[sub]
            beta_col = cols[:, heads + head : heads + head + 1]
            exp_col = cols[:, 2 * heads + head : 2 * heads + head + 1]
            keyed = keyed_ref[sub * key_heads + head // group]
            value = feat_ref[sub, :, head * DV : (head + 1) * DV]
            right.append(beside(keyed * (beta_col * exp_col), value * beta_col))
        for sub, head in both:
            item = sub * heads + head
            inv = (inv_ref[2 * item, 0], inv_ref[2 * item, 1])
            tops.append(split(product(inv, split(right[item][:HALF]))))
        for sub, head in both:
            item = sub * heads + head
            rest = right[item][HALF:] - product((below_ref[item, 0], below_ref[item, 1]), tops[item])
            inv = (inv_ref[2 * item + 1, 0], inv_ref[2 * item + 1, 1])
            lows.append(split(product(inv, split(rest))))
        for sub, head in both:
            item = sub * heads + head
            solved = (above(tops[item][0], lows[item][0]), above(tops[item][1], lows[item][1]))
            solved_out[group_at * GROUP + sub, head, 0] = solved[0]
            solved_out[group_at * GROUP + sub, head, 1] = solved[1]
            cum_row = cum_ref[sub, head : head + 1]
            last = cum_row[:, SPAN - 1 : SPAN]
            faded = split(turned_ref[sub * key_heads + head // group] * jnp.exp(last - cum_row))
            gathered = product(faded, solved)
            maps = unit * jnp.exp(last) - gathered[:, :DK]
            map_ref[sub, head] = beside(*split(maps))
            add_ref[sub, head] = gathered[:, DK:]

    def one_round(group_at, carried):
        follow(jnp.maximum(group_at - 2, 0))
        solve(group_at - 1)
        prepare(group_at)
        return carried

    rounds = spans // GROUP
    prepare(0)
    lax.fori_loop(1, rounds, one_round, 0)
    follow(rounds - 2)
    solve(rounds - 1)
    follow(rounds - 1)
    turn = turn_ref[0]
    for place, end_ref in enumerate((end0, end1, end2, end3)):
        end_ref[...] = fin_ref[lax.rem(turn + place, heads)]


def query_kernel(
    query_ref, halo_ref, taps_ref, keyt_ref, solved_ref, start_ref, row_ref, col_ref, *rest
):
    local_out, carry_out, begin, finish = rest[-4:]
    width = query_ref.shape[1]
    key_heads = width // DK
    heads = solved_ref.shape[1]
    group = heads // key_heads
    halo = halo_ref[:, :width]

    def one_span(span, carried):
        here = pl.ds(span * SPAN, SPAN)
        ahead = pl.ds(max(span * SPAN - 16, 0), 16)
        feat = conv_silu(halo, query_ref[ahead, :], query_ref[here, :], taps_ref[...], span == 0)
        cum_rows = row_ref[:, here]
        cols = col_ref[here, :]
        queries, grams = [], []
        for key_head in range(key_heads):
            query = feat[:, key_head * DK : (key_head + 1) * DK]
            queries.append(query)
            grams.append(product(split(query), (keyt_ref[span, key_head, 0], keyt_ref[span, key_head, 1])))
        lifted = []
        for head in range(heads):
            gram = grams[head // group]
            top, low, end = decay_blocks(cols[:, head : head + 1], cum_rows[head : head + 1], False)
            high, fine = solved_ref[span, head, 0], solved_ref[span, head, 1]
            upper = product(split(gram[:HALF, :HALF] * top), (high[:HALF], fine[:HALF]))
            wide = beside(gram[HALF:, :HALF] * low, gram[HALF:, HALF:] * end)
            lifted.append(above(upper, product(split(wide), (high, fine))))
        for head in range(heads):
            exp_col = cols[:, 2 * heads + head : 2 * heads + head + 1]
            reach = queries[head // group] * exp_col - lifted[head][:, :DK]
            seen = product(split(reach), (start_ref[span, head, 0], start_ref[span, head, 1]))
            local_out[here, head * DV : (head + 1) * DV] = seen[:, :DV] + lifted[head][:, DK:]
            carry_out[here, head * 2 * DK : (head + 1) * 2 * DK] = beside(*split(seen[:, DV:]))
        return carried

    for span in range(begin, finish):
        one_span(span, 0)


def pack_kernel(query_ref, key_ref, val_ref, out_ref):
    out_ref[...] = beside(query_ref[...], key_ref[...], val_ref[...])


def compose_kernel(turn_ref, part0, part1, part2, part3, total_out, tail_out, prefix_out, all_ref):
    count = all_ref.shape[0]
    turn = turn_ref[0]
    for place, part in enumerate((part0, part1, part2, part3)):
        all_ref[lax.rem(turn + count - place, count)] = part[...]
    running = all_ref[0]
    prefix_out[0] = running
    for member in range(1, count):
        own = all_ref[member]
        moved = product(split(own[:, DV:]), split(running))
        running = beside(moved[:, :DV] + own[:, :DV], moved[:, DV:])
        if member < count - 1:
            prefix_out[member] = running
    total_out[...] = running
    tail_out[...] = running[:, :DV]


def enter_kernel(turn_ref, place_ref, near_ref, next_ref, far_ref, prefix_ref, out0, out1, out2, out3, all_ref):
    count = all_ref.shape[0]
    turn = turn_ref[0]
    place = place_ref[0]
    near, following, far = (
        jnp.where(place >= back, ref[...], 0.0)
        for back, ref in ((1, near_ref), (2, next_ref), (3, far_ref))
    )
    far = following[:, :DV] + product_small(split(following[:, DV:]), split(far))
    entry = near[:, :DV] + product_small(split(near[:, DV:]), split(far))
    parts = split(entry)
    all_ref[0] = entry
    for member in range(1, count):
        prefix = prefix_ref[member - 1]
        all_ref[member] = prefix[:, :DV] + product_small(split(prefix[:, DV:]), parts)
    for place, out in enumerate((out0, out1, out2, out3)):
        out[...] = all_ref[lax.rem(turn + place, count)]


def close_kernel(
    turn_ref, part0, part1, part2, part3, local_ref, carry_ref, gain_ref, out_ref, state_ref, done_ref, sems
):
    heads = state_ref.shape[0]
    turn = turn_ref[0]
    for place, part in enumerate((part0, part1, part2, part3)):
        pair = beside(*split(part[...]))
        state_ref[lax.rem(turn + heads - place, heads)] = above(pair, pair)
    spans = local_ref.shape[0] // SPAN

    def copy_out(span):
        here = pl.ds(span * SPAN, SPAN)
        return pltpu.make_async_copy(done_ref.at[here, :], out_ref.at[here, :], sems.at[span])

    def one_span(span, carried):
        here = pl.ds(span * SPAN, SPAN)
        for head in range(heads):
            both = dot(carry_ref[here, head * 2 * DK : (head + 1) * 2 * DK], state_ref[head])
            value = local_ref[here, head * DV : (head + 1) * DV] + both[:, :DV] + both[:, DV:]
            scale = lax.rsqrt(jnp.sum(value * value, axis=1, keepdims=True) * (1.0 / DV) + 1e-6)
            gain = gain_ref[:, head * DV : (head + 1) * DV]
            done_ref[here, head * DV : (head + 1) * DV] = (value * scale * gain).astype(bf16)
        copy_out(span).start()
        return carried

    def finish(span, carried):
        copy_out(span).wait()
        return carried

    for span in range(spans):
        one_span(span, 0)
    for span in range(spans):
        finish(span, 0)


def whole(shape):
    return pl.BlockSpec(shape, lambda *_: (0,) * len(shape))


def params(mebibytes):
    return pltpu.CompilerParams(dimension_semantics=("arbitrary",), vmem_limit_bytes=mebibytes * MIB)


def cost(flops, size, exps=0):
    return pl.CostEstimate(flops=flops, bytes_accessed=size, transcendentals=exps)


def per_device(
    query_in, key_in, value_in, log_decay, beta_gate, conv_query, conv_key, conv_value, norm_gain
):
    tok_rows, query_width = query_in.shape
    value_width = value_in.shape[1]
    key_heads = query_width // DK
    heads = value_width // DV
    spans = tok_rows // SPAN
    turn = lax.axis_index("outer").astype(jnp.int32).reshape(1)
    place = lax.axis_index("inner").astype(jnp.int32).reshape(1)
    far_in = tuple(
        pltpu.with_memory_space_constraint(array, pltpu.HBM) for array in (query_in, key_in, value_in)
    )
    tail_block = tok_rows // 16 - 1
    all_width = 2 * query_width + value_width
    tails = pl.pallas_call(
        pack_kernel,
        grid=(1,),
        in_specs=[
            pl.BlockSpec((16, query_width), lambda i: (tail_block, 0)),
            pl.BlockSpec((16, query_width), lambda i: (tail_block, 0)),
            pl.BlockSpec((16, value_width), lambda i: (tail_block, 0)),
        ],
        out_specs=whole((16, all_width)),
        out_shape=jax.ShapeDtypeStruct((16, all_width), bf16),
        compiler_params=params(4),
        cost_estimate=cost(0, 64_000),
        name="pack",
    )(*far_in)
    before = shifted(tails, ("inner", "outer"), 1, False)
    gates = above(log_decay.T, beta_gate.T)

    square = jax.ShapeDtypeStruct((DK, 2 * DV), f32)
    keyt, solved, starts, rows, cols, *ends = pl.pallas_call(
        state_kernel,
        grid_spec=pltpu.PrefetchScalarGridSpec(
            num_scalar_prefetch=1,
            grid=(),
            in_specs=[pl.BlockSpec(memory_space=pltpu.VMEM)] * 6,
            out_specs=[pl.BlockSpec(memory_space=pltpu.VMEM)] * 9,
            scratch_shapes=[
                pltpu.VMEM((heads, 2, DK, 2 * DV), bf16),
                pltpu.VMEM((GROUP, heads, DK, 2 * DK), bf16),
                pltpu.VMEM((GROUP, heads, DK, DV), f32),
                pltpu.VMEM((heads, DK, 2 * DV), f32),
                pltpu.VMEM((3, HALF, HALF), bf16),
                pltpu.VMEM((2 * HALF, (BASE - 1) * HALF), bf16),
                pltpu.VMEM((SPAN, SPAN), bf16),
                pltpu.VMEM((2 * GROUP * heads, 2, HALF, HALF), bf16),
                pltpu.VMEM((GROUP * heads, 2, HALF, HALF), bf16),
                pltpu.VMEM((GROUP * key_heads, SPAN, DK), f32),
                pltpu.VMEM((GROUP * key_heads, DK, SPAN), f32),
                pltpu.VMEM((GROUP, SPAN, value_width), f32),
                pltpu.VMEM((GROUP, SPAN, HALF), f32),
                pltpu.VMEM((GROUP, 2 * heads, SPAN), f32),
            ],
        ),
        out_shape=[
            jax.ShapeDtypeStruct((spans, key_heads, 2, DK, SPAN), bf16),
            jax.ShapeDtypeStruct((spans, heads, 2, SPAN, 2 * DV), bf16),
            jax.ShapeDtypeStruct((spans, heads, 2, DK, 2 * DV), bf16),
            jax.ShapeDtypeStruct((2 * heads, tok_rows), f32),
            jax.ShapeDtypeStruct((tok_rows, HALF), f32),
        ]
        + [square] * 4,
        compiler_params=pltpu.CompilerParams(vmem_limit_bytes=STATE_MIB * MIB),
        cost_estimate=cost(20_000_000_000, 20_000_000),
        name="state_path",
    )(turn, before, key_in, value_in, gates, conv_key, conv_value)

    parts = [ends[0]] + [shifted(ends[k], "outer", k, True) for k in (1, 2, 3)]

    out_types = (
        jax.ShapeDtypeStruct((tok_rows, value_width), f32),
        jax.ShapeDtypeStruct((tok_rows, 2 * value_width), bf16),
    )

    def query_part(offset, count, earlier):
        def body(*refs):
            query_kernel(*refs, offset, offset + count)

        return pl.pallas_call(
            body,
            in_specs=[pl.BlockSpec(memory_space=pltpu.VMEM)] * (8 + len(earlier)),
            out_specs=[pl.BlockSpec(memory_space=pltpu.VMEM)] * 2,
            out_shape=out_types,
            input_output_aliases={8 + k: k for k in range(len(earlier))},
            compiler_params=pltpu.CompilerParams(vmem_limit_bytes=QUERY_MIB * MIB),
            cost_estimate=cost(2_000_000_000 * count, 3_000_000 * count),
            name="query_path",
        )(query_in, before, conv_query, keyt, solved, starts, rows, cols, *earlier)

    cuts = (0, (3 * spans) // 8, (5 * spans) // 8, spans)
    seen = query_part(cuts[0], cuts[1] - cuts[0], ())
    parts, seen = lax.optimization_barrier((parts, seen))

    total, tail, prefix = pl.pallas_call(
        compose_kernel,
        grid_spec=pltpu.PrefetchScalarGridSpec(
            num_scalar_prefetch=1,
            grid=(1,),
            in_specs=[whole((DK, 2 * DV))] * 4,
            out_specs=[whole((DK, 2 * DV)), whole((DK, DV)), whole((3, DK, 2 * DV))],
            scratch_shapes=[pltpu.VMEM((4, DK, 2 * DV), f32)],
        ),
        out_shape=[
            square,
            jax.ShapeDtypeStruct((DK, DV), f32),
            jax.ShapeDtypeStruct((3, DK, 2 * DV), f32),
        ],
        compiler_params=params(8),
        cost_estimate=cost(100_000_000, 1_000_000),
        name="compose",
    )(turn, *parts)
    near = shifted(total, "inner", 1, True)
    middle = shifted(total, "inner", 2, True)
    far = shifted(tail, "inner", 3, True)

    seen = query_part(cuts[1], cuts[2] - cuts[1], seen)
    near, seen = lax.optimization_barrier((near, seen))
    local, carry = query_part(cuts[2], cuts[3] - cuts[2], seen)

    entries = pl.pallas_call(
        enter_kernel,
        grid_spec=pltpu.PrefetchScalarGridSpec(
            num_scalar_prefetch=2,
            grid=(1,),
            in_specs=[whole((DK, 2 * DV)), whole((DK, 2 * DV)), whole((DK, DV)), whole((3, DK, 2 * DV))],
            out_specs=[whole((DK, DV))] * 4,
            scratch_shapes=[pltpu.VMEM((4, DK, DV), f32)],
        ),
        out_shape=[jax.ShapeDtypeStruct((DK, DV), f32)] * 4,
        compiler_params=params(8),
        cost_estimate=cost(50_000_000, 1_000_000),
        name="enter",
    )(turn, place, near, middle, far, prefix)
    states = [entries[0]] + [shifted(entries[k], "outer", k, True) for k in (1, 2, 3)]

    return pl.pallas_call(
        close_kernel,
        grid_spec=pltpu.PrefetchScalarGridSpec(
            num_scalar_prefetch=1,
            grid=(),
            in_specs=[pl.BlockSpec(memory_space=pltpu.VMEM)] * 7,
            out_specs=pl.BlockSpec(memory_space=pltpu.HBM),
            scratch_shapes=[
                pltpu.VMEM((heads, 2 * DK, 2 * DV), bf16),
                pltpu.VMEM((tok_rows, value_width), bf16),
                pltpu.SemaphoreType.DMA((spans,)),
            ],
        ),
        out_shape=jax.ShapeDtypeStruct((tok_rows, value_width), bf16),
        compiler_params=pltpu.CompilerParams(vmem_limit_bytes=12 * MIB),
        cost_estimate=cost(2_000_000_000, 10_000_000),
        name="close",
    )(turn, *states, local, carry, norm_gain.reshape(1, value_width))


def solution(mesh):
    in_specs = (
        P(("inner", "outer"), "head"),
        P(("inner", "outer"), "head"),
        P(("inner", "outer"), "head"),
        P(("inner", "outer"), "head"),
        P(("inner", "outer"), "head"),
        P(None, "head"),
        P(None, "head"),
        P(None, "head"),
        P("head"),
    )
    out_specs = P(("inner", "outer"), "head")
    return jax.shard_map(
        per_device, mesh=mesh, in_specs=in_specs, out_specs=out_specs, check_vma=False
    )
```

```python
import jax
import jax.numpy as jnp
from jax import lax
from jax.experimental import pallas as pl
from jax.experimental.pallas import tpu as pltpu
from jax.sharding import PartitionSpec as P

DK = 128
DV = 128
CONV = 4
SPAN = 256
HALF = 128
BASE = 16
GROUP = 2
MIB = 1024 * 1024
STATE_MIB = 24
QUERY_MIB = 14

f32 = jnp.float32
bf16 = jnp.bfloat16


def shifted(value, axis, steps, wrap):
    count = lax.axis_size(axis)
    if wrap:
        pairs = [(source, (source + steps) % count) for source in range(count)]
    else:
        pairs = [(source, source + steps) for source in range(count - steps)]
    return lax.ppermute(value, axis, pairs)


def split(value):
    high = value.astype(bf16)
    return high, (value - high.astype(f32)).astype(bf16)


def dot(left, right):
    return jnp.dot(left, right, preferred_element_type=f32)


def beside(*parts):
    return jnp.concatenate(parts, axis=1)


def above(*parts):
    return jnp.concatenate(parts, axis=0)


def product(left, right):
    if left[0].shape[1] == HALF:
        return dot(beside(*left), above(right[0], right[0])) + dot(left[0], right[1])
    return dot(left[0], right[0]) + dot(left[1], right[0]) + dot(left[0], right[1])


def product_small(left, right):
    return dot(beside(*left), above(right[0], right[0])) + dot(left[0], right[1])


def odd_rows(value, size):
    return above(*(value[start : start + size] for start in range(size, value.shape[0], 2 * size)))


def spread_rows(value, size):
    gap = jnp.zeros((size, value.shape[1]), value.dtype)
    return above(*(part for start in range(0, value.shape[0], size) for part in (gap, value[start : start + size])))


def merge_rows(value, odd, size):
    return above(
        *(
            part
            for start in range(0, odd.shape[0], size)
            for part in (value[2 * start : 2 * start + size], odd[start : start + size])
        )
    )


def iotas(shape):
    return lax.broadcasted_iota(jnp.int32, shape, 0), lax.broadcasted_iota(jnp.int32, shape, 1)


def conv_silu(halo, prev, cur, taps, first):
    prev = jnp.where(first, halo.astype(f32), prev.astype(f32))
    cur = cur.astype(f32)
    taps = taps.astype(f32)
    extended = above(prev[8:], cur)
    rows = cur.shape[0]
    total = taps[CONV - 1 : CONV] * cur
    for tap in range(CONV - 1):
        start = 8 - (CONV - 1) + tap
        total = total + taps[tap : tap + 1] * extended[start : start + rows]
    return total / (1.0 + jnp.exp(-total))


def decay_blocks(cum_col, cum_row, strict):
    row_ids, col_ids = iotas((HALF, HALF))
    keep = (row_ids > col_ids) if strict else (row_ids >= col_ids)
    top = jnp.exp(jnp.where(keep, cum_col[:HALF] - cum_row[:, :HALF], -1e30))
    low = jnp.exp(cum_col[HALF:] - cum_row[:, :HALF])
    end = jnp.exp(jnp.where(keep, cum_col[HALF:] - cum_row[:, HALF:], -1e30))
    return top, low, end


def state_kernel(
    turn_ref, halo_ref, key_ref, val_ref, gate_ref, key_taps, val_taps,
    keyt_out, solved_out, start_out, row_out, col_out, end0, end1, end2, end3,
    run_ref, map_ref, add_ref, fin_ref, level_ref, pick_ref, tri_ref,
    inv_ref, below_ref, keyed_ref, turned_ref, feat_ref, held_ref, cum_ref,
):
    heads = run_ref.shape[0]
    width = key_ref.shape[1]
    key_heads = width // DK
    spans = key_ref.shape[0] // SPAN
    halo = halo_ref[...]
    group = heads // key_heads
    row_ids, col_ids = iotas((HALF, HALF))
    unit = jnp.where(row_ids == col_ids, 1.0, 0.0).astype(f32)
    base_mask = (row_ids // BASE) == (col_ids // BASE)

    zeros = jnp.zeros((HALF, HALF), f32)
    for head in range(heads):
        run_ref[head, 0] = beside(zeros, unit).astype(bf16)
        run_ref[head, 1] = beside(zeros, zeros).astype(bf16)
        for sub in range(GROUP):
            map_ref[sub, head] = beside(unit, zeros).astype(bf16)
            add_ref[sub, head] = zeros
    size = BASE
    for level in range(level_ref.shape[0]):
        picked = (
            (row_ids // (2 * size) == col_ids // (2 * size))
            & (row_ids % (2 * size) >= size)
            & (col_ids % (2 * size) < size)
        )
        level_ref[level] = jnp.where(picked, 1.0, 0.0).astype(bf16)
        size *= 2
    for place in range(BASE - 1):
        chosen = jnp.where(row_ids == (col_ids // BASE) * BASE + place, 1.0, 0.0).astype(bf16)
        pick_ref[:, place * HALF : (place + 1) * HALF] = above(chosen, chosen)
    tri_rows, tri_cols = iotas((SPAN, SPAN))
    tri_ref[...] = jnp.where(tri_rows <= tri_cols, 1.0, 0.0).astype(bf16)

    def advance(head, sub, high, low):
        maps = map_ref[sub, head]
        moved = dot(maps, above(high, high)) + dot(maps[:, :DK], low)
        return beside(moved[:, :DV] + add_ref[sub, head], moved[:, DV:])

    def follow(group_at):
        for head in range(heads):
            high, low = run_ref[head, 0], run_ref[head, 1]
            for sub in range(GROUP):
                start_out[group_at * GROUP + sub, head, 0] = high
                start_out[group_at * GROUP + sub, head, 1] = low
                reached = advance(head, sub, high, low)
                high, low = split(reached)
            run_ref[head, 0] = high
            run_ref[head, 1] = low
            fin_ref[head] = reached

    def prepare(group_at):
        feats = []
        for sub in range(GROUP):
            span = group_at * GROUP + sub
            here = pl.ds(span * SPAN, SPAN)
            ahead = pl.ds(max(span * SPAN - 16, 0), 16)
            gates = gate_ref[:, here]
            is_log = lax.broadcasted_iota(jnp.int32, gates.shape, 0) < heads
            logs = jnp.where(is_log, gates, 0.0)
            logs = above(logs, logs)
            high = logs.astype(bf16)
            rest = logs - high.astype(f32)
            mid = rest.astype(bf16)
            low = (rest - mid.astype(f32)).astype(bf16)
            tri = tri_ref[...]
            cum = (dot(high, tri) + dot(mid, tri) + dot(low, tri))[: gates.shape[0]]
            row_out[:, here] = cum
            packed = above(
                jnp.where(is_log, cum, gates),
                jnp.exp(cum),
                jnp.zeros((HALF - 2 * gates.shape[0], SPAN), f32),
            )
            cols = packed.T
            col_out[here, :] = cols
            first = span == 0
            key_feat = conv_silu(
                halo[:, width : 2 * width], key_ref[ahead, :], key_ref[here, :], key_taps[...], first
            )
            val_feat = conv_silu(
                halo[:, 2 * width :], val_ref[ahead, :], val_ref[here, :], val_taps[...], first
            )
            feats.append((span, cum, cols, key_feat, val_feat))

        diag, below, keyed_all = [], [], []
        for span, cum, cols, key_feat, _ in feats:
            grams = []
            for key_head in range(key_heads):
                feat = key_feat[:, key_head * DK : (key_head + 1) * DK]
                keyed = feat * lax.rsqrt(jnp.sum(feat * feat, axis=1, keepdims=True) + 1e-6)
                turned = keyed.T
                parts = split(turned)
                keyt_out[span, key_head, 0] = parts[0]
                keyt_out[span, key_head, 1] = parts[1]
                keyed_all.append((keyed, turned))
                grams.append(product(split(keyed), parts))
            for head in range(heads):
                gram = grams[head // group]
                beta_col = cols[:, heads + head : heads + head + 1]
                top, low, end = decay_blocks(cols[:, head : head + 1], cum[head : head + 1], True)
                diag.append(gram[:HALF, :HALF] * top * beta_col[:HALF])
                below.append(split(gram[HALF:, :HALF] * low * beta_col[HALF:]))
                diag.append(gram[HALF:, HALF:] * end * beta_col[HALF:])

        blocks = HALF // BASE
        compact = above(
            *(jnp.sum(jnp.where(base_mask, item, 0.0).reshape(blocks, BASE, HALF), axis=0) for item in diag)
        )
        spread = dot(beside(*split(compact)), pick_ref[...])
        count = len(diag)
        within = lax.broadcasted_iota(jnp.int32, (count, BASE, HALF), 1)
        lanes = lax.broadcasted_iota(jnp.int32, (count, BASE, HALF), 2)
        small = jnp.where(within == lanes % BASE, 1.0, 0.0).astype(f32)
        for place in range(BASE - 1):
            factor = spread[:, place * HALF : (place + 1) * HALF].reshape(count, BASE, HALF)
            small = small - factor * small[:, place : place + 1, :]
        inverses = [
            jnp.where(
                base_mask, jnp.broadcast_to(small[item][None], (blocks, BASE, HALF)).reshape(HALF, HALF), 0.0
            )
            for item in range(count)
        ]
        diag_parts = [split(item) for item in diag]
        size = BASE
        inv_parts = [split(item) for item in inverses]
        for level in range(level_ref.shape[0]):
            mask = odd_rows(level_ref[level], size)
            odd_parts = [tuple(odd_rows(part, size) for part in inv) for inv in inv_parts]
            inner = [
                product_small(tuple(odd_rows(part, size) * mask for part in item), inv)
                for item, inv in zip(diag_parts, inv_parts)
            ]
            fresh = [
                odd_rows(item, size) - product_small(odd, tuple(spread_rows(part, size) for part in split(part_in)))
                for item, odd, part_in in zip(inverses, odd_parts, inner)
            ]
            inv_parts = [
                tuple(merge_rows(old, new, size) for old, new in zip(inv, split(item)))
                for inv, item in zip(inv_parts, fresh)
            ]
            inverses = [merge_rows(old, new, size) for old, new in zip(inverses, fresh)]
            size *= 2

        for item in range(count):
            inv_ref[item, 0], inv_ref[item, 1] = inv_parts[item]
        for item, parts in enumerate(below):
            below_ref[item, 0], below_ref[item, 1] = parts
        for item, (keyed, turned) in enumerate(keyed_all):
            keyed_ref[item] = keyed
            turned_ref[item] = turned
        for sub, (_, cum, cols, _, val_feat) in enumerate(feats):
            feat_ref[sub] = val_feat
            held_ref[sub] = cols
            cum_ref[sub] = cum

    def solve(group_at):
        both = [(sub, head) for sub in range(GROUP) for head in range(heads)]
        tops, lows, right = [], [], []
        for sub, head in both:
            cols = held_ref[sub]
            beta_col = cols[:, heads + head : heads + head + 1]
            exp_col = cols[:, 2 * heads + head : 2 * heads + head + 1]
            keyed = keyed_ref[sub * key_heads + head // group]
            value = feat_ref[sub, :, head * DV : (head + 1) * DV]
            right.append(beside(keyed * (beta_col * exp_col), value * beta_col))
        for sub, head in both:
            item = sub * heads + head
            inv = (inv_ref[2 * item, 0], inv_ref[2 * item, 1])
            tops.append(split(product(inv, split(right[item][:HALF]))))
        for sub, head in both:
            item = sub * heads + head
            rest = right[item][HALF:] - product((below_ref[item, 0], below_ref[item, 1]), tops[item])
            inv = (inv_ref[2 * item + 1, 0], inv_ref[2 * item + 1, 1])
            lows.append(split(product(inv, split(rest))))
        for sub, head in both:
            item = sub * heads + head
            solved = (above(tops[item][0], lows[item][0]), above(tops[item][1], lows[item][1]))
            solved_out[group_at * GROUP + sub, head, 0] = solved[0]
            solved_out[group_at * GROUP + sub, head, 1] = solved[1]
            cum_row = cum_ref[sub, head : head + 1]
            last = cum_row[:, SPAN - 1 : SPAN]
            faded = split(turned_ref[sub * key_heads + head // group] * jnp.exp(last - cum_row))
            gathered = product(faded, solved)
            maps = unit * jnp.exp(last) - gathered[:, :DK]
            map_ref[sub, head] = beside(*split(maps))
            add_ref[sub, head] = gathered[:, DK:]

    def one_round(group_at, carried):
        if group_at > 1:
            follow(group_at - 2)
        solve(group_at - 1)
        prepare(group_at)
        return carried

    rounds = spans // GROUP
    prepare(0)
    for group_at in range(1, rounds):
        one_round(group_at, 0)
    follow(rounds - 2)
    solve(rounds - 1)
    follow(rounds - 1)
    turn = turn_ref[0]
    for place, end_ref in enumerate((end0, end1, end2, end3)):
        end_ref[...] = fin_ref[lax.rem(turn + place, heads)]


def query_kernel(
    query_ref, halo_ref, taps_ref, keyt_ref, solved_ref, start_ref, row_ref, col_ref, *rest
):
    local_out, carry_out, begin, finish = rest[-4:]
    width = query_ref.shape[1]
    key_heads = width // DK
    heads = solved_ref.shape[1]
    group = heads // key_heads
    halo = halo_ref[:, :width]

    def one_span(span, carried):
        here = pl.ds(span * SPAN, SPAN)
        ahead = pl.ds(max(span * SPAN - 16, 0), 16)
        feat = conv_silu(halo, query_ref[ahead, :], query_ref[here, :], taps_ref[...], span == 0)
        cum_rows = row_ref[:, here]
        cols = col_ref[here, :]
        queries, grams = [], []
        for key_head in range(key_heads):
            query = feat[:, key_head * DK : (key_head + 1) * DK]
            queries.append(query)
            grams.append(product(split(query), (keyt_ref[span, key_head, 0], keyt_ref[span, key_head, 1])))
        lifted = []
        for head in range(heads):
            gram = grams[head // group]
            top, low, end = decay_blocks(cols[:, head : head + 1], cum_rows[head : head + 1], False)
            high, fine = solved_ref[span, head, 0], solved_ref[span, head, 1]
            upper = product(split(gram[:HALF, :HALF] * top), (high[:HALF], fine[:HALF]))
            wide = beside(gram[HALF:, :HALF] * low, gram[HALF:, HALF:] * end)
            lifted.append(above(upper, product(split(wide), (high, fine))))
        for head in range(heads):
            exp_col = cols[:, 2 * heads + head : 2 * heads + head + 1]
            reach = queries[head // group] * exp_col - lifted[head][:, :DK]
            seen = product(split(reach), (start_ref[span, head, 0], start_ref[span, head, 1]))
            local_out[here, head * DV : (head + 1) * DV] = seen[:, :DV] + lifted[head][:, DK:]
            carry_out[here, head * 2 * DK : (head + 1) * 2 * DK] = beside(*split(seen[:, DV:]))
        return carried

    for span in range(begin, finish):
        one_span(span, 0)


def pack_kernel(query_ref, key_ref, val_ref, out_ref):
    out_ref[...] = beside(query_ref[...], key_ref[...], val_ref[...])


def compose_kernel(turn_ref, part0, part1, part2, part3, total_out, tail_out, prefix_out, all_ref):
    count = all_ref.shape[0]
    turn = turn_ref[0]
    for place, part in enumerate((part0, part1, part2, part3)):
        all_ref[lax.rem(turn + count - place, count)] = part[...]
    running = all_ref[0]
    prefix_out[0] = running
    for member in range(1, count):
        own = all_ref[member]
        moved = product(split(own[:, DV:]), split(running))
        running = beside(moved[:, :DV] + own[:, :DV], moved[:, DV:])
        if member < count - 1:
            prefix_out[member] = running
    total_out[...] = running
    tail_out[...] = running[:, :DV]


def enter_kernel(turn_ref, place_ref, near_ref, next_ref, far_ref, prefix_ref, out0, out1, out2, out3, all_ref):
    count = all_ref.shape[0]
    turn = turn_ref[0]
    place = place_ref[0]
    near, following, far = (
        jnp.where(place >= back, ref[...], 0.0)
        for back, ref in ((1, near_ref), (2, next_ref), (3, far_ref))
    )
    far = following[:, :DV] + product_small(split(following[:, DV:]), split(far))
    entry = near[:, :DV] + product_small(split(near[:, DV:]), split(far))
    parts = split(entry)
    all_ref[0] = entry
    for member in range(1, count):
        prefix = prefix_ref[member - 1]
        all_ref[member] = prefix[:, :DV] + product_small(split(prefix[:, DV:]), parts)
    for place, out in enumerate((out0, out1, out2, out3)):
        out[...] = all_ref[lax.rem(turn + place, count)]


def close_kernel(
    turn_ref, part0, part1, part2, part3, local_ref, carry_ref, gain_ref, out_ref, state_ref, done_ref, sems
):
    heads = state_ref.shape[0]
    turn = turn_ref[0]
    for place, part in enumerate((part0, part1, part2, part3)):
        pair = beside(*split(part[...]))
        state_ref[lax.rem(turn + heads - place, heads)] = above(pair, pair)
    spans = local_ref.shape[0] // SPAN

    def copy_out(span):
        here = pl.ds(span * SPAN, SPAN)
        return pltpu.make_async_copy(done_ref.at[here, :], out_ref.at[here, :], sems.at[span])

    def one_span(span, carried):
        here = pl.ds(span * SPAN, SPAN)
        for head in range(heads):
            both = dot(carry_ref[here, head * 2 * DK : (head + 1) * 2 * DK], state_ref[head])
            value = local_ref[here, head * DV : (head + 1) * DV] + both[:, :DV] + both[:, DV:]
            scale = lax.rsqrt(jnp.sum(value * value, axis=1, keepdims=True) * (1.0 / DV) + 1e-6)
            gain = gain_ref[:, head * DV : (head + 1) * DV]
            done_ref[here, head * DV : (head + 1) * DV] = (value * scale * gain).astype(bf16)
        copy_out(span).start()
        return carried

    def finish(span, carried):
        copy_out(span).wait()
        return carried

    for span in range(spans):
        one_span(span, 0)
    for span in range(spans):
        finish(span, 0)


def whole(shape):
    return pl.BlockSpec(shape, lambda *_: (0,) * len(shape))


def params(mebibytes):
    return pltpu.CompilerParams(dimension_semantics=("arbitrary",), vmem_limit_bytes=mebibytes * MIB)


def cost(flops, size, exps=0):
    return pl.CostEstimate(flops=flops, bytes_accessed=size, transcendentals=exps)


def per_device(
    query_in, key_in, value_in, log_decay, beta_gate, conv_query, conv_key, conv_value, norm_gain
):
    tok_rows, query_width = query_in.shape
    value_width = value_in.shape[1]
    key_heads = query_width // DK
    heads = value_width // DV
    spans = tok_rows // SPAN
    turn = lax.axis_index("outer").astype(jnp.int32).reshape(1)
    place = lax.axis_index("inner").astype(jnp.int32).reshape(1)
    far_in = tuple(
        pltpu.with_memory_space_constraint(array, pltpu.HBM) for array in (query_in, key_in, value_in)
    )
    tail_block = tok_rows // 16 - 1
    all_width = 2 * query_width + value_width
    tails = pl.pallas_call(
        pack_kernel,
        grid=(1,),
        in_specs=[
            pl.BlockSpec((16, query_width), lambda i: (tail_block, 0)),
            pl.BlockSpec((16, query_width), lambda i: (tail_block, 0)),
            pl.BlockSpec((16, value_width), lambda i: (tail_block, 0)),
        ],
        out_specs=whole((16, all_width)),
        out_shape=jax.ShapeDtypeStruct((16, all_width), bf16),
        compiler_params=params(4),
        cost_estimate=cost(0, 64_000),
        name="pack",
    )(*far_in)
    before = shifted(tails, ("inner", "outer"), 1, False)
    gates = above(log_decay.T, beta_gate.T)

    square = jax.ShapeDtypeStruct((DK, 2 * DV), f32)
    keyt, solved, starts, rows, cols, *ends = pl.pallas_call(
        state_kernel,
        grid_spec=pltpu.PrefetchScalarGridSpec(
            num_scalar_prefetch=1,
            grid=(),
            in_specs=[pl.BlockSpec(memory_space=pltpu.VMEM)] * 6,
            out_specs=[pl.BlockSpec(memory_space=pltpu.VMEM)] * 9,
            scratch_shapes=[
                pltpu.VMEM((heads, 2, DK, 2 * DV), bf16),
                pltpu.VMEM((GROUP, heads, DK, 2 * DK), bf16),
                pltpu.VMEM((GROUP, heads, DK, DV), f32),
                pltpu.VMEM((heads, DK, 2 * DV), f32),
                pltpu.VMEM((3, HALF, HALF), bf16),
                pltpu.VMEM((2 * HALF, (BASE - 1) * HALF), bf16),
                pltpu.VMEM((SPAN, SPAN), bf16),
                pltpu.VMEM((2 * GROUP * heads, 2, HALF, HALF), bf16),
                pltpu.VMEM((GROUP * heads, 2, HALF, HALF), bf16),
                pltpu.VMEM((GROUP * key_heads, SPAN, DK), f32),
                pltpu.VMEM((GROUP * key_heads, DK, SPAN), f32),
                pltpu.VMEM((GROUP, SPAN, value_width), f32),
                pltpu.VMEM((GROUP, SPAN, HALF), f32),
                pltpu.VMEM((GROUP, 2 * heads, SPAN), f32),
            ],
        ),
        out_shape=[
            jax.ShapeDtypeStruct((spans, key_heads, 2, DK, SPAN), bf16),
            jax.ShapeDtypeStruct((spans, heads, 2, SPAN, 2 * DV), bf16),
            jax.ShapeDtypeStruct((spans, heads, 2, DK, 2 * DV), bf16),
            jax.ShapeDtypeStruct((2 * heads, tok_rows), f32),
            jax.ShapeDtypeStruct((tok_rows, HALF), f32),
        ]
        + [square] * 4,
        compiler_params=pltpu.CompilerParams(vmem_limit_bytes=STATE_MIB * MIB),
        cost_estimate=cost(20_000_000_000, 20_000_000),
        name="state_path",
    )(turn, before, key_in, value_in, gates, conv_key, conv_value)

    parts = [ends[0]] + [shifted(ends[k], "outer", k, True) for k in (1, 2, 3)]

    out_types = (
        jax.ShapeDtypeStruct((tok_rows, value_width), f32),
        jax.ShapeDtypeStruct((tok_rows, 2 * value_width), bf16),
    )

    def query_part(offset, count, earlier):
        def body(*refs):
            query_kernel(*refs, offset, offset + count)

        return pl.pallas_call(
            body,
            in_specs=[pl.BlockSpec(memory_space=pltpu.VMEM)] * (8 + len(earlier)),
            out_specs=[pl.BlockSpec(memory_space=pltpu.VMEM)] * 2,
            out_shape=out_types,
            input_output_aliases={8 + k: k for k in range(len(earlier))},
            compiler_params=pltpu.CompilerParams(vmem_limit_bytes=QUERY_MIB * MIB),
            cost_estimate=cost(2_000_000_000 * count, 3_000_000 * count),
            name="query_path",
        )(query_in, before, conv_query, keyt, solved, starts, rows, cols, *earlier)

    cuts = (0, (3 * spans) // 8, (5 * spans) // 8, spans)
    seen = query_part(cuts[0], cuts[1] - cuts[0], ())
    parts, seen = lax.optimization_barrier((parts, seen))

    total, tail, prefix = pl.pallas_call(
        compose_kernel,
        grid_spec=pltpu.PrefetchScalarGridSpec(
            num_scalar_prefetch=1,
            grid=(1,),
            in_specs=[whole((DK, 2 * DV))] * 4,
            out_specs=[whole((DK, 2 * DV)), whole((DK, DV)), whole((3, DK, 2 * DV))],
            scratch_shapes=[pltpu.VMEM((4, DK, 2 * DV), f32)],
        ),
        out_shape=[
            square,
            jax.ShapeDtypeStruct((DK, DV), f32),
            jax.ShapeDtypeStruct((3, DK, 2 * DV), f32),
        ],
        compiler_params=params(8),
        cost_estimate=cost(100_000_000, 1_000_000),
        name="compose",
    )(turn, *parts)
    near = shifted(total, "inner", 1, True)
    middle = shifted(total, "inner", 2, True)
    far = shifted(tail, "inner", 3, True)

    seen = query_part(cuts[1], cuts[2] - cuts[1], seen)
    near, seen = lax.optimization_barrier((near, seen))
    local, carry = query_part(cuts[2], cuts[3] - cuts[2], seen)

    entries = pl.pallas_call(
        enter_kernel,
        grid_spec=pltpu.PrefetchScalarGridSpec(
            num_scalar_prefetch=2,
            grid=(1,),
            in_specs=[whole((DK, 2 * DV)), whole((DK, 2 * DV)), whole((DK, DV)), whole((3, DK, 2 * DV))],
            out_specs=[whole((DK, DV))] * 4,
            scratch_shapes=[pltpu.VMEM((4, DK, DV), f32)],
        ),
        out_shape=[jax.ShapeDtypeStruct((DK, DV), f32)] * 4,
        compiler_params=params(8),
        cost_estimate=cost(50_000_000, 1_000_000),
        name="enter",
    )(turn, place, near, middle, far, prefix)
    states = [entries[0]] + [shifted(entries[k], "outer", k, True) for k in (1, 2, 3)]

    return pl.pallas_call(
        close_kernel,
        grid_spec=pltpu.PrefetchScalarGridSpec(
            num_scalar_prefetch=1,
            grid=(),
            in_specs=[pl.BlockSpec(memory_space=pltpu.VMEM)] * 7,
            out_specs=pl.BlockSpec(memory_space=pltpu.HBM),
            scratch_shapes=[
                pltpu.VMEM((heads, 2 * DK, 2 * DV), bf16),
                pltpu.VMEM((tok_rows, value_width), bf16),
                pltpu.SemaphoreType.DMA((spans,)),
            ],
        ),
        out_shape=jax.ShapeDtypeStruct((tok_rows, value_width), bf16),
        compiler_params=pltpu.CompilerParams(vmem_limit_bytes=12 * MIB),
        cost_estimate=cost(2_000_000_000, 10_000_000),
        name="close",
    )(turn, *states, local, carry, norm_gain.reshape(1, value_width))


def solution(mesh):
    in_specs = (
        P(("inner", "outer"), "head"),
        P(("inner", "outer"), "head"),
        P(("inner", "outer"), "head"),
        P(("inner", "outer"), "head"),
        P(("inner", "outer"), "head"),
        P(None, "head"),
        P(None, "head"),
        P(None, "head"),
        P("head"),
    )
    out_specs = P(("inner", "outer"), "head")
    return jax.shard_map(
        per_device, mesh=mesh, in_specs=in_specs, out_specs=out_specs, check_vma=False
    )
```
